32 devices in a mesh: dom: 8 (over y, x, core), cls: 4 (over z).
Axes of the slice: x: 2, y: 2, z: 4, core: 2. Of those that a mesh axis runs over, the one named last changes fastest.
Arguments:
- particles: bfloat16 [512, 16384], P(('dom', 'cls')), may hold values from -6 to 6
- averages: float32 [128, 16384], P('cls'), may hold values from -4 to 4
- prior_mass: float32 [128], P('cls'), may hold values from 1 to 8
- group_ids: int32 [4, 512, 1], P(None, ('dom', 'cls')), may hold values from 0 to 3; in each aligned block of 16 rows (0 to 15, 16 to 31, ..., all dimensions but the last counted through in order) at most 6 rows name the same one
- class_ids: int32 [4, 512], P(None, ('dom', 'cls')), may hold values from 0 to 31
- rot_ids: int32 [4, 512], P(None, ('dom', 'cls')), may hold values from 0 to 63
- weights: bfloat16 [4, 512], P(None, ('dom', 'cls')), may hold values from 0.25 to 4
- owners: int32 [4], replicated, may hold values from 0 to 3
Outputs:
- scores: float32 [4, 512, 2048], P(None, ('dom', 'cls'))
- final_averages: float32 [128, 16384], P('cls')
The draws below stay inside these ranges and needn't reach their ends.
Inputs may be any that keep to these rules, and one draw needn't show every extreme that they name: `group_ids`: in every step, at most 6 of the 16 particles of one device name one class group; in every step some device's particles reach 6 for some group.
All inputs are finite; a program needn't handle non-finite values.
Results may differ from the reference program's by a relative error of at most 0.0027.
Values may be sent and summed in bfloat16 or wider, within the bound.
A program may use at most 256 MiB of HBM per device.

```python
import math
import jax
import jax.numpy as jnp
import numpy as np
from jax import lax

RADII = 128
ANGLES = 128
ROT = 64
CLS_DEV = 32
PD = 16
STEPS = 4
CAP = 6
ASTEP = 2
CLASSES = 128
PARTICLES = 512
N_CLS = 4


def with_ends(drawn, rng, low, largest):
    longest = drawn.shape.index(max(drawn.shape))
    spots = []
    for shift in (0, 1):
        where = [jax.random.randint(jax.random.fold_in(rng, axis), (), 0, length) for axis, length in enumerate(drawn.shape)]
        where[longest] = (where[longest] + shift) % drawn.shape[longest]
        spots.append(tuple(where))
    return drawn.at[spots[0]].set(low).at[spots[1]].set(largest)


def level_of(stream_key, shape, shards, low, high):
    loudness, own = 1.0, jax.random.fold_in(stream_key, 6)
    for dim, blocks in shards:
        steps = jnp.exp(jax.random.uniform(jax.random.fold_in(own, dim), (blocks,), jnp.float32, low / len(shards), high / len(shards)))
        loudness = loudness * jnp.repeat(steps, shape[dim] // blocks).reshape([-1 if axis == dim else 1 for axis in range(len(shape))])
    return loudness


def cumulative_ranks(count, slope):
    portions = [(1 << 20) // math.isqrt(standing ** slope) + 1 for standing in range(1, count + 1)]
    spread = 1 + sum(portions) // (1 << 30)
    return np.cumsum(np.array([max(1, weight // spread) for weight in portions]))


def ranked_ids(own_key, dims, number_of, slope):
    listing = cumulative_ranks(number_of, slope)
    lot = jax.random.randint(jax.random.fold_in(own_key, 1), dims, 0, int(listing[number_of - 1]))
    grade = jnp.searchsorted(jnp.asarray(listing, jnp.int32), lot, side="right")
    return jax.random.permutation(jax.random.fold_in(own_key, 2), number_of)[grade].astype(jnp.int32)


def routed_block(key, own, number, rows, amount, top, bound, skew):
    ranking = jax.random.permutation(key, amount)
    crowded, common = portions_of(amount, rows * top, bound, skew, True), portions_of(amount, rows * top, bound, skew, False)
    places = jnp.arange(amount)

    def named(lengths, turn):
        used = int((lengths > 0).sum())
        fixed = max(1, used // 4)
        passed = fixed + (places - fixed + turn * (used - fixed)) % max(1, amount - fixed)
        return jnp.zeros((amount,), jnp.int32).at[ranking[jnp.where(places < fixed, places, passed)]].set(jnp.asarray(lengths, jnp.int32))

    lengths = jnp.where(number % 4 == 0, named(crowded, number // 4), named(common, number - number // 4 - 1))
    mixed = jax.random.permutation(jax.random.fold_in(own, 3), amount)
    donor, sink = mixed[0:amount // 2 * 2:2], mixed[1:amount // 2 * 2:2]
    slack = jnp.minimum(lengths[donor] - 1, bound - lengths[sink]) // 2
    slack = jnp.where((donor == ranking[0]) | (sink == ranking[0]) | (lengths[sink] == 0), 0, jnp.maximum(slack, 0))
    passed = jax.random.randint(jax.random.fold_in(own, 4), (amount // 2,), 0, 1 << 20) % (slack + 1)
    lengths = lengths.at[donor].add(-passed).at[sink].add(passed)
    items = jnp.searchsorted(jnp.cumsum(lengths), jnp.arange(rows * top), side="right").astype(jnp.int32)
    listing = items.reshape(top, rows).T
    listing = listing[jax.random.permutation(jax.random.fold_in(own, 1), rows)]
    turn = jax.random.randint(jax.random.fold_in(own, 2), (rows, 1), 0, top)
    return jnp.take_along_axis(listing, (jnp.arange(top)[None, :] + turn) % top, axis=1)


def portions_of(amount, total, bound, lean, full):
    weights = [(1 << 20) // math.isqrt(grade ** lean) + 1 for grade in range(1, amount + 1)]
    largest = bound if full else min(bound, max(-(-total // amount), total * weights[0] // sum(weights)))
    least = 1 if total - largest >= amount - 1 else 0
    holding, surplus = [largest] + [least] * (amount - 1), total - largest - least * (amount - 1)
    while surplus > 0:
        free = [i for i in range(1, amount) if holding[i] < largest] or [i for i in range(1, amount) if holding[i] < bound]
        pool, left = sum([weights[i] for i in free]), surplus
        for i in free:
            addition = min(bound - holding[i], max(1, left * weights[i] // pool), surplus)
            holding[i] = holding[i] + addition
            surplus = surplus - addition
    return np.array(holding)


def centred(own_key, dims, width, bound, shards=(), held_as=jnp.bfloat16):
    values = width * jax.random.normal(own_key, dims, jnp.float32)
    if shards:
        values = values * level_of(own_key, dims, shards, -0.22, 0.18)
    return jnp.clip(values, -bound, bound).astype(held_as)


def setup_inputs(seed: int = 0) -> dict:
    keys = jax.random.split(jax.random.key(seed), 9)
    particles = centred(keys[0], (PARTICLES, RADII * ANGLES), 1.0, 6.0, ((0, 32),))
    averages = centred(keys[1], (CLASSES, RADII * ANGLES), 0.5, 4.0, ((0, 4),), jnp.float32)
    prior_mass = jnp.clip(jnp.exp(math.log(8.0) - 2.0794415 * jax.random.uniform(keys[2], (CLASSES,), jnp.float32) ** level_of(keys[2], (CLASSES,), ((0, 4),), -0.2, 0.2)), 1.0, 8.0)
    group_ids_keys = jax.random.split(jax.random.fold_in(keys[3], 1), STEPS * PARTICLES // PD)
    group_ids_turns = jax.random.permutation(jax.random.fold_in(keys[3], 3), STEPS * PARTICLES // PD)
    group_ids = jax.vmap(lambda own, number: routed_block(jax.random.fold_in(keys[3], 2), own, number, PD, N_CLS, 1, CAP, 2))(group_ids_keys, group_ids_turns).reshape((STEPS, PARTICLES, 1))
    class_ids = with_ends(ranked_ids(keys[4], (STEPS, PARTICLES), CLS_DEV, 2), jax.random.fold_in(keys[4], 3), 0, CLS_DEV - 1).astype(jnp.int32)
    rot_ids = with_ends(jax.random.randint(keys[5], (STEPS, PARTICLES), 0, ROT), jax.random.fold_in(keys[5], 1), 0, ROT - 1).astype(jnp.int32)
    weights = jnp.clip(jnp.exp(math.log(4.0) - 2.7725887 * jax.random.uniform(keys[6], (STEPS, PARTICLES), jnp.float32) ** level_of(keys[6], (STEPS, PARTICLES), ((1, 32),), -0.2, 0.2)), 0.25, 4.0).astype(jnp.bfloat16)
    owners = with_ends(jax.random.randint(keys[7], (STEPS,), 0, N_CLS), jax.random.fold_in(keys[7], 1), 0, N_CLS - 1).astype(jnp.int32)
    return dict(particles=particles, averages=averages, prior_mass=prior_mass, group_ids=group_ids, class_ids=class_ids, rot_ids=rot_ids, weights=weights, owners=owners)


def rotate_each(images, shifts):
    angle_idx = jnp.arange(ANGLES, dtype=jnp.int32)
    index = (angle_idx[None, :] - shifts[:, None]) % ANGLES
    return jnp.take_along_axis(images, index[:, None, :], axis=2)

def reference(particles, averages, prior_mass, group_ids, class_ids, rot_ids, weights, owners):
    pixels = RADII * ANGLES
    cube = particles.reshape(-1, RADII, ANGLES)
    flat = particles
    scale = 1.0 / math.sqrt(pixels)
    current = averages
    all_scores = []
    for step in range(STEPS):
        shifts = (rot_ids[step] * ASTEP).astype(jnp.int32)
        rotated = rotate_each(cube, shifts).reshape(-1, pixels)
        labels = (group_ids[step, :, 0] * CLS_DEV + class_ids[step]).astype(jnp.int32)
        wts = weights[step].astype(jnp.float32)
        terms = rotated.astype(jnp.float32) * wts[:, None]
        totals = jax.ops.segment_sum(terms, labels, num_segments=CLASSES)
        mass = jax.ops.segment_sum(wts, labels, num_segments=CLASSES)
        current = (prior_mass[:, None] * current + totals) / (prior_mass + mass)[:, None]
        start = (owners[step] * CLS_DEV).astype(jnp.int32)
        refs = lax.dynamic_slice_in_dim(current, start, CLS_DEV, 0).astype(jnp.bfloat16)
        ref_cube = refs.reshape(CLS_DEV, RADII, ANGLES)
        blocks = []
        for turn in range(ROT):
            turned = jnp.roll(ref_cube, -turn * ASTEP, axis=2).reshape(CLS_DEV, pixels)
            blocks.append(jnp.dot(flat, turned.T, preferred_element_type=jnp.float32))
        stacked = jnp.stack(blocks, axis=1).reshape(cube.shape[0], ROT * CLS_DEV)
        all_scores.append(stacked * scale)
    return (jnp.stack(all_scores, axis=0), current)
```

```python
import functools
import math

import jax
import jax.numpy as jnp
from jax import lax
from jax.experimental import pallas as pl
from jax.experimental.pallas import tpu as pltpu
from jax.sharding import PartitionSpec as P

RADII = 128
ANGLES = 128
ROT = 64
STEPS = 4
ASTEP = 2
MIB = 1024 * 1024


def update_kernel(owners_ref, parts_ref, av_ref, label_ref, weight_ref, shift_ref, prior_ref, refs_ref, final_ref):
    count, width = parts_ref.shape
    classes = av_ref.shape[0]
    per_group = refs_ref.shape[0] // STEPS
    radii = width // ANGLES
    prior = prior_ref[...]
    lane = lax.broadcasted_iota(jnp.int32, (count, ANGLES), 1)
    class_row = lax.broadcasted_iota(jnp.int32, (classes, count), 0)
    final_ref[...] = av_ref[...]
    for step in range(STEPS):
        index = (lane - shift_ref[:, step : step + 1]) & (ANGLES - 1)
        hot = jnp.where(class_row == label_ref[step : step + 1, :], weight_ref[step : step + 1, :], 0.0)
        mass = jnp.sum(hot, axis=1, keepdims=True)
        hot = hot.astype(jnp.bfloat16)
        inverse = 1.0 / (prior + mass)
        for a in range(radii):
            cols = slice(a * ANGLES, (a + 1) * ANGLES)
            image = parts_ref[:, cols].astype(jnp.float32)
            turned = jnp.take_along_axis(image, index, axis=1).astype(jnp.bfloat16)
            totals = jnp.dot(hot, turned, preferred_element_type=jnp.float32)
            final_ref[:, cols] = (prior * final_ref[:, cols] + totals) * inverse
        start = pl.multiple_of(owners_ref[step] * per_group, per_group)
        refs_ref[step * per_group : (step + 1) * per_group, :] = final_ref[pl.ds(start, per_group), :].astype(
            jnp.bfloat16
        )


def score_kernel(parts_ref, refs_ref, out_ref, rolled, total):
    step = pl.program_id(0)
    per_dev = parts_ref.shape[0]
    blocks, names, width = refs_ref.shape
    per_group = names // STEPS
    radii = parts_ref.shape[1] // ANGLES
    for a in range(radii):
        cols = slice(a * ANGLES, (a + 1) * ANGLES)
        image = parts_ref[:, cols]
        for r in range(ROT):
            turned = pltpu.roll(image, r * ASTEP, 1) if r else image
            rolled[r * per_dev : (r + 1) * per_dev, cols] = turned
    product = None
    for b in range(blocks):
        part = lax.dot_general(
            rolled[:, b * width : (b + 1) * width],
            refs_ref[b],
            (((1,), (1,)), ((), ())),
            preferred_element_type=jnp.float32,
        )
        product = part if product is None else product + part

    @pl.when(step == 0)
    def _():
        total[...] = product

    @pl.when(step > 0)
    def _():
        total[...] += product

    @pl.when(step == pl.num_programs(0) - 1)
    def _():
        scale = 1.0 / math.sqrt(RADII * ANGLES)
        pack = 128 // per_group
        for q in range(ROT // pack):
            tiles = [total[(q * pack + j) * per_dev : (q * pack + j + 1) * per_dev, :] * scale for j in range(pack)]
            for s in range(STEPS):
                out_ref[s, :, q * 128 : (q + 1) * 128] = jnp.concatenate(
                    [t[:, s * per_group : (s + 1) * per_group] for t in tiles], axis=1
                )


def per_device(particles, averages, prior_mass, group_ids, class_ids, rot_ids, weights, owners):
    per_dev, pixels = particles.shape
    per_group = averages.shape[0]
    doms, groups = lax.axis_size("dom"), lax.axis_size("cls")
    devices = doms * groups
    width = pixels // devices
    count = per_dev * devices
    classes = per_group * groups
    everywhere = ("dom", "cls")

    label = (group_ids[:, :, 0] * per_group + class_ids).astype(jnp.float32)
    shift = (rot_ids * ASTEP).astype(jnp.float32)
    meta = jnp.stack([label, shift, weights.astype(jnp.float32)])
    flat = jnp.concatenate([meta.reshape(-1), prior_mass])
    gathered = lax.all_gather(flat, everywhere, axis=0, tiled=False)
    size = 3 * STEPS * per_dev
    meta = gathered[:, :size].reshape(devices, 3, STEPS, per_dev).transpose(1, 2, 0, 3).reshape(3, STEPS, count)
    prior = gathered[:groups, size:].reshape(classes, 1)

    mine = lax.all_to_all(
        particles.reshape(per_dev, devices, width).transpose(1, 0, 2), everywhere, split_axis=0, concat_axis=0, tiled=True
    ).reshape(count, width)
    band = lax.dynamic_slice_in_dim(averages, lax.axis_index("dom") * groups * width, groups * width, 1)
    band = lax.all_to_all(
        band.reshape(per_group, groups, width).transpose(1, 0, 2), "cls", split_axis=0, concat_axis=0, tiled=True
    ).reshape(classes, width)

    vmem = pl.BlockSpec(memory_space=pltpu.VMEM)
    refs, final = pl.pallas_call(
        update_kernel,
        out_shape=(
            jax.ShapeDtypeStruct((STEPS * per_group, width), jnp.bfloat16),
            jax.ShapeDtypeStruct((classes, width), jnp.float32),
        ),
        in_specs=[pl.BlockSpec(memory_space=pltpu.SMEM)] + [vmem] * 6,
        out_specs=(vmem, vmem),
        compiler_params=pltpu.CompilerParams(vmem_limit_bytes=40 * MIB),
        name="update",
    )(owners, mine, band, meta[0].astype(jnp.int32), meta[2], meta[1].astype(jnp.int32).T, prior)

    all_refs = lax.all_gather(refs, everywhere, axis=0, tiled=False)
    last = lax.all_to_all(
        final.astype(jnp.bfloat16).reshape(groups, per_group, width), "cls", split_axis=0, concat_axis=0, tiled=True
    )
    last = lax.all_gather(last, "dom", axis=0, tiled=False)
    last = last.transpose(2, 0, 1, 3).reshape(per_group, pixels).astype(jnp.float32)

    chunks = 8
    scores = pl.pallas_call(
        score_kernel,
        grid=(chunks,),
        out_shape=jax.ShapeDtypeStruct((STEPS, per_dev, ROT * per_group), jnp.float32),
        in_specs=[
            pl.BlockSpec((per_dev, pixels // chunks), lambda c: (0, c)),
            pl.BlockSpec((devices // chunks, STEPS * per_group, width), lambda c: (c, 0, 0)),
        ],
        out_specs=pl.BlockSpec((STEPS, per_dev, ROT * per_group), lambda c: (0, 0, 0)),
        scratch_shapes=[
            pltpu.VMEM((ROT * per_dev, pixels // chunks), jnp.bfloat16),
            pltpu.VMEM((ROT * per_dev, STEPS * per_group), jnp.float32),
        ],
        compiler_params=pltpu.CompilerParams(vmem_limit_bytes=40 * MIB),
        name="scores",
    )(particles, all_refs)
    return scores, last


def solution(mesh):
    return jax.shard_map(
        per_device,
        mesh=mesh,
        in_specs=(
            P(("dom", "cls"), None),
            P("cls", None),
            P("cls"),
            P(None, ("dom", "cls"), None),
            P(None, ("dom", "cls")),
            P(None, ("dom", "cls")),
            P(None, ("dom", "cls")),
            P(),
        ),
        out_specs=(P(None, ("dom", "cls"), None), P("cls", None)),
        check_vma=False,
    )
```

```python
import functools
import math

import jax
import jax.numpy as jnp
from jax import lax
from jax.experimental import pallas as pl
from jax.experimental.pallas import tpu as pltpu
from jax.sharding import PartitionSpec as P

RADII = 128
ANGLES = 128
ROT = 64
STEPS = 4
ASTEP = 2
MIB = 1024 * 1024


def update_kernel(owners_ref, parts_ref, av_ref, label_ref, weight_ref, shift_ref, prior_ref, refs_ref, last_ref, current):
    senders, rows = parts_ref.shape[:2]
    groups, padded, width = av_ref.shape
    per_group = last_ref.shape[1]
    radii = width // ANGLES
    per_dev = rows // (radii + 1)
    count, classes = senders * per_dev, groups * per_group
    prior = prior_ref[...]
    lane = lax.broadcasted_iota(jnp.int32, (count, ANGLES), 1)
    class_row = lax.broadcasted_iota(jnp.int32, (classes, count), 0)
    current[...] = av_ref[:, :per_group, :].reshape(classes, width)
    for step in range(STEPS):
        index = (lane - shift_ref[:, step : step + 1]) & (ANGLES - 1)
        hot = jnp.where(class_row == label_ref[step : step + 1, :], weight_ref[step : step + 1, :], 0.0)
        mass = jnp.sum(hot, axis=1, keepdims=True)
        hot = hot.astype(jnp.bfloat16)
        inverse = 1.0 / (prior + mass)
        for a in range(radii):
            cols = slice(a * ANGLES, (a + 1) * ANGLES)
            image = parts_ref[:, a * per_dev : (a + 1) * per_dev, :].reshape(count, ANGLES).astype(jnp.float32)
            turned = jnp.take_along_axis(image, index, axis=1).astype(jnp.bfloat16)
            totals = jnp.dot(hot, turned, preferred_element_type=jnp.float32)
            current[:, cols] = (prior * current[:, cols] + totals) * inverse
        start = pl.multiple_of(owners_ref[step] * per_group, per_group)
        refs_ref[step * per_group : (step + 1) * per_group, :] = current[pl.ds(start, per_group), :].astype(jnp.bfloat16)
    last_ref[...] = current[...].astype(jnp.bfloat16).reshape(groups, per_group, width)


def gather_kernel(doms, groups, refs_ref, final_ref, slots_ref, last_ref, own_sem, z_send, z_recv, d_send, d_recv):
    dom, cls = lax.axis_index("dom"), lax.axis_index("cls")
    bits = doms.bit_length() - 1
    per_group, width = final_ref.shape[1:]

    def across(bit):
        return dom + (1 << bit) - (2 << bit) * (lax.div(dom, 1 << bit) % 2)

    def peer(hop):
        return lax.rem(cls + hop, groups)

    barrier = pltpu.get_barrier_semaphore()
    for hop in range(1, groups):
        pl.semaphore_signal(barrier, device_id={"dom": dom, "cls": peer(hop)}, device_id_type=pl.DeviceIdType.MESH)
    for bit in range(bits):
        pl.semaphore_signal(barrier, device_id={"dom": across(bit), "cls": cls}, device_id_type=pl.DeviceIdType.MESH)
    pl.semaphore_wait(barrier, groups - 1 + bits)

    def columns(which_dom, which_cls, count):
        return pl.ds(pl.multiple_of((which_dom * groups + which_cls) * width, width), count * width)

    own = [
        pltpu.make_async_copy(refs_ref, slots_ref.at[dom, cls], own_sem.at[0]),
        pltpu.make_async_copy(final_ref.at[cls], last_ref.at[:, columns(dom, cls, 1)], own_sem.at[1]),
    ]
    sent = []
    for hop in range(1, groups):
        target = {"dom": dom, "cls": peer(hop)}
        moves = [
            pltpu.make_async_remote_copy(
                refs_ref, slots_ref.at[dom, cls], z_send.at[0, hop], z_recv.at[0, hop], target, pl.DeviceIdType.MESH
            ),
            pltpu.make_async_remote_copy(
                final_ref.at[peer(hop)],
                last_ref.at[:, columns(dom, cls, 1)],
                z_send.at[1, hop],
                z_recv.at[1, hop],
                target,
                pl.DeviceIdType.MESH,
            ),
        ]
        for move in moves:
            move.start()
        sent.extend(moves)
    for copy in own:
        copy.start()
    for copy in own:
        copy.wait()
    for move in sent:
        move.wait_recv()

    def part(half, which_dom):
        span = groups // 2
        rows = per_group // 2
        return (
            slots_ref.at[which_dom, half * span : (half + 1) * span],
            last_ref.at[half * rows : (half + 1) * rows, columns(which_dom, 0, groups)],
        )

    orders = [list(range(1, bits)) + [0], list(range(bits - 1, 0, -1)) + [0]]
    for stage in range(bits):
        moves = []
        for half, order in enumerate(orders):
            bit = order[stage]
            done = order[:stage]
            target = {"dom": across(bit), "cls": cls}
            for pick in range(1 << stage):
                slot = dom
                for place, old in enumerate(done):
                    if pick >> place & 1:
                        slot = slot + (1 << old) - (2 << old) * (lax.div(dom, 1 << old) % 2)
                for kind, piece in enumerate(part(half, slot)):
                    spot = (1 << stage) - 1 + pick
                    moves.append(
                        pltpu.make_async_remote_copy(
                            piece,
                            piece,
                            d_send.at[half, kind, spot],
                            d_recv.at[half, kind, spot],
                            target,
                            pl.DeviceIdType.MESH,
                        )
                    )
        for move in moves:
            move.start()
        for move in moves:
            move.wait_recv()
        sent.extend(moves)
    for move in sent:
        move.wait_send()


def score_kernel(parts_ref, refs_ref, out_ref, rolled, total):
    step = pl.program_id(0)
    per_dev = parts_ref.shape[0]
    blocks, names, width = refs_ref.shape
    per_group = names // STEPS
    radii = parts_ref.shape[1] // ANGLES
    for a in range(radii):
        cols = slice(a * ANGLES, (a + 1) * ANGLES)
        image = parts_ref[:, cols]
        for r in range(ROT):
            turned = pltpu.roll(image, r * ASTEP, 1) if r else image
            rolled[r * per_dev : (r + 1) * per_dev, cols] = turned
    product = None
    for b in range(blocks):
        part = lax.dot_general(
            rolled[:, b * width : (b + 1) * width],
            refs_ref[b],
            (((1,), (1,)), ((), ())),
            preferred_element_type=jnp.float32,
        )
        product = part if product is None else product + part

    @pl.when(step == 0)
    def _():
        total[...] = product

    @pl.when(step > 0)
    def _():
        total[...] += product

    @pl.when(step == pl.num_programs(0) - 1)
    def _():
        scale = 1.0 / math.sqrt(RADII * ANGLES)
        pack = 128 // per_group
        for q in range(ROT // pack):
            tiles = [total[(q * pack + j) * per_dev : (q * pack + j + 1) * per_dev, :] * scale for j in range(pack)]
            for s in range(STEPS):
                out_ref[s, :, q * 128 : (q + 1) * 128] = jnp.concatenate(
                    [t[:, s * per_group : (s + 1) * per_group] for t in tiles], axis=1
                )


def per_device(particles, averages, prior_mass, group_ids, class_ids, rot_ids, weights, owners):
    per_dev, pixels = particles.shape
    per_group = averages.shape[0]
    doms, groups = lax.axis_size("dom"), lax.axis_size("cls")
    devices = doms * groups
    width = pixels // devices
    radii = width // ANGLES
    count = per_dev * devices
    classes = per_group * groups

    meta = jnp.stack([group_ids[:, :, 0], class_ids, rot_ids]).astype(jnp.bfloat16)
    meta = jnp.concatenate([meta, weights[None]]).reshape(-1)
    size = meta.shape[0]
    meta = jnp.pad(meta, (0, per_dev * ANGLES - size)).reshape(1, per_dev, ANGLES)
    blocks = particles.reshape(per_dev, devices, radii, ANGLES).transpose(1, 2, 0, 3)
    blocks = blocks.reshape(devices, radii * per_dev, ANGLES)
    blocks = jnp.concatenate([blocks, jnp.broadcast_to(meta, (devices, per_dev, ANGLES))], axis=1)
    mine = lax.all_to_all(blocks, ("dom", "cls"), split_axis=0, concat_axis=0, tiled=True)

    band = lax.dynamic_slice_in_dim(averages, lax.axis_index("dom") * groups * width, groups * width, 1)
    band = band.reshape(per_group, groups, width).transpose(1, 0, 2)
    extra = jnp.pad(prior_mass, (0, 8 * width - per_group)).reshape(1, 8, width)
    band = jnp.concatenate([band, jnp.broadcast_to(extra, (groups, 8, width))], axis=1)
    band = lax.all_to_all(band, "cls", split_axis=0, concat_axis=0, tiled=True)
    prior = band[:, per_group, :per_group].reshape(classes, 1)

    meta = mine[:, radii * per_dev :, :].reshape(devices, per_dev * ANGLES)[:, :size]
    meta = meta.reshape(devices, 4, STEPS, per_dev).transpose(1, 2, 0, 3).reshape(4, STEPS, count).astype(jnp.float32)
    label = (meta[0] * per_group + meta[1]).astype(jnp.int32)
    shift = (meta[2] * ASTEP).astype(jnp.int32).T

    vmem = pl.BlockSpec(memory_space=pltpu.VMEM)
    refs, final = pl.pallas_call(
        update_kernel,
        out_shape=(
            jax.ShapeDtypeStruct((STEPS * per_group, width), jnp.bfloat16),
            jax.ShapeDtypeStruct((groups, per_group, width), jnp.bfloat16),
        ),
        in_specs=[pl.BlockSpec(memory_space=pltpu.SMEM)] + [vmem] * 6,
        out_specs=(vmem, vmem),
        scratch_shapes=[pltpu.VMEM((classes, width), jnp.float32)],
        compiler_params=pltpu.CompilerParams(vmem_limit_bytes=40 * MIB),
        name="update",
    )(owners, mine, band, label, meta[3], shift, prior)

    hbm = pl.BlockSpec(memory_space=pl.ANY)
    dma = pltpu.SemaphoreType.DMA
    all_refs, last = pl.pallas_call(
        functools.partial(gather_kernel, doms, groups),
        out_shape=(
            jax.ShapeDtypeStruct((doms, groups, STEPS * per_group, width), jnp.bfloat16),
            jax.ShapeDtypeStruct((per_group, pixels), jnp.bfloat16),
        ),
        in_specs=[hbm, hbm],
        out_specs=(hbm, hbm),
        scratch_shapes=[
            dma((2,)),
            dma((2, groups)),
            dma((2, groups)),
            dma((2, 2, doms)),
            dma((2, 2, doms)),
        ],
        compiler_params=pltpu.CompilerParams(collective_id=0, has_side_effects=True),
        name="gather",
    )(refs, final)
    all_refs = all_refs.reshape(devices, STEPS * per_group, width)
    last = last.astype(jnp.float32)

    chunks = 8
    scores = pl.pallas_call(
        score_kernel,
        grid=(chunks,),
        out_shape=jax.ShapeDtypeStruct((STEPS, per_dev, ROT * per_group), jnp.float32),
        in_specs=[
            pl.BlockSpec((per_dev, pixels // chunks), lambda c: (0, c)),
            pl.BlockSpec((devices // chunks, STEPS * per_group, width), lambda c: (c, 0, 0)),
        ],
        out_specs=pl.BlockSpec((STEPS, per_dev, ROT * per_group), lambda c: (0, 0, 0)),
        scratch_shapes=[
            pltpu.VMEM((ROT * per_dev, pixels // chunks), jnp.bfloat16),
            pltpu.VMEM((ROT * per_dev, STEPS * per_group), jnp.float32),
        ],
        compiler_params=pltpu.CompilerParams(vmem_limit_bytes=40 * MIB),
        name="scores",
    )(particles, all_refs)
    return scores, last


def solution(mesh):
    return jax.shard_map(
        per_device,
        mesh=mesh,
        in_specs=(
            P(("dom", "cls"), None),
            P("cls", None),
            P("cls"),
            P(None, ("dom", "cls"), None),
            P(None, ("dom", "cls")),
            P(None, ("dom", "cls")),
            P(None, ("dom", "cls")),
            P(),
        ),
        out_specs=(P(None, ("dom", "cls"), None), P("cls", None)),
        check_vma=False,
    )
```

```python
import functools
import math

import jax
import jax.numpy as jnp
from jax import lax
from jax.experimental import pallas as pl
from jax.experimental.pallas import tpu as pltpu
from jax.sharding import PartitionSpec as P

RADII = 128
ANGLES = 128
ROT = 64
STEPS = 4
ASTEP = 2
MIB = 1024 * 1024


def update_kernel(owners_ref, parts_ref, av_ref, label_ref, weight_ref, shift_ref, prior_ref, refs_ref, last_ref, current):
    senders, rows = parts_ref.shape[:2]
    groups, padded, width = av_ref.shape
    per_group = last_ref.shape[1]
    radii = width // ANGLES
    per_dev = rows // (radii + 1)
    count, classes = senders * per_dev, groups * per_group
    prior = prior_ref[...]
    lane = lax.broadcasted_iota(jnp.int32, (count, ANGLES), 1)
    class_row = lax.broadcasted_iota(jnp.int32, (classes, count), 0)
    current[...] = av_ref[:, :per_group, :].reshape(classes, width)
    for step in range(STEPS):
        index = (lane - shift_ref[:, step : step + 1]) & (ANGLES - 1)
        hot = jnp.where(class_row == label_ref[step : step + 1, :], weight_ref[step : step + 1, :], 0.0)
        mass = jnp.sum(hot, axis=1, keepdims=True)
        hot = hot.astype(jnp.bfloat16)
        inverse = 1.0 / (prior + mass)
        for a in range(radii):
            cols = slice(a * ANGLES, (a + 1) * ANGLES)
            image = parts_ref[:, a * per_dev : (a + 1) * per_dev, :].reshape(count, ANGLES).astype(jnp.float32)
            turned = jnp.take_along_axis(image, index, axis=1).astype(jnp.bfloat16)
            totals = jnp.dot(hot, turned, preferred_element_type=jnp.float32)
            current[:, cols] = (prior * current[:, cols] + totals) * inverse
        start = pl.multiple_of(owners_ref[step] * per_group, per_group)
        refs_ref[step * per_group : (step + 1) * per_group, :] = current[pl.ds(start, per_group), :].astype(jnp.bfloat16)
    last_ref[...] = current[...].astype(jnp.bfloat16).reshape(groups, per_group, width)


def exchange_kernel(doms, groups, blocks_ref, band_ref, mine_ref, got_ref, own_sem, send, recv, b_send, b_recv):
    dom, cls = lax.axis_index("dom"), lax.axis_index("cls")
    devices = doms * groups
    me = dom * groups + cls

    def peer(hop):
        return lax.rem(me + hop, devices)

    def place(device):
        return {"dom": lax.div(device, groups), "cls": lax.rem(device, groups)}

    barrier = pltpu.get_barrier_semaphore()

    @pl.loop(1, devices)
    def _(hop):
        pl.semaphore_signal(barrier, device_id=place(peer(hop)), device_id_type=pl.DeviceIdType.MESH)

    pl.semaphore_wait(barrier, devices - 1)

    def block(hop):
        return pltpu.make_async_remote_copy(
            blocks_ref.at[peer(hop)],
            mine_ref.at[me],
            send.at[hop],
            recv.at[hop],
            place(peer(hop)),
            pl.DeviceIdType.MESH,
        )

    def band(hop):
        other = lax.rem(cls + hop, groups)
        return pltpu.make_async_remote_copy(
            band_ref.at[other],
            got_ref.at[cls],
            b_send.at[hop],
            b_recv.at[hop],
            {"dom": dom, "cls": other},
            pl.DeviceIdType.MESH,
        )

    @pl.loop(1, devices)
    def _(hop):
        block(hop).start()

    @pl.loop(1, groups)
    def _(hop):
        band(hop).start()

    own = [
        pltpu.make_async_copy(blocks_ref.at[me], mine_ref.at[me], own_sem.at[0]),
        pltpu.make_async_copy(band_ref.at[cls], got_ref.at[cls], own_sem.at[1]),
    ]
    for copy in own:
        copy.start()
    for copy in own:
        copy.wait()

    @pl.loop(1, devices)
    def _(hop):
        block(hop).wait()

    @pl.loop(1, groups)
    def _(hop):
        band(hop).wait()


def gather_kernel(doms, groups, refs_ref, final_ref, slots_ref, last_ref, own_sem, z_send, z_recv, r_send, r_recv, f_send, f_recv):
    dom, cls = lax.axis_index("dom"), lax.axis_index("cls")
    bits = doms.bit_length() - 1
    per_group, width = final_ref.shape[1:]

    def across(bit):
        return dom + (1 << bit) - (2 << bit) * (lax.div(dom, 1 << bit) % 2)

    def peer(hop):
        return lax.rem(cls + hop, groups)

    barrier = pltpu.get_barrier_semaphore()
    for hop in range(1, groups):
        pl.semaphore_signal(barrier, device_id={"dom": dom, "cls": peer(hop)}, device_id_type=pl.DeviceIdType.MESH)
    for bit in range(bits):
        pl.semaphore_signal(barrier, device_id={"dom": across(bit), "cls": cls}, device_id_type=pl.DeviceIdType.MESH)
    pl.semaphore_wait(barrier, groups - 1 + bits)

    def columns(which_dom, which_cls, count):
        return pl.ds(pl.multiple_of((which_dom * groups + which_cls) * width, width), count * width)

    half_rows = (refs_ref.shape[0] // 2, per_group // 2)
    own = [
        pltpu.make_async_copy(refs_ref, slots_ref.at[dom, cls], own_sem.at[0]),
        pltpu.make_async_copy(final_ref.at[cls], last_ref.at[:, columns(dom, cls, 1)], own_sem.at[1]),
    ]
    for copy in own:
        copy.start()
    z_refs, z_last = [], []
    for hop in range(1, groups):
        target = {"dom": dom, "cls": peer(hop)}
        z_refs.append(
            pltpu.make_async_remote_copy(
                refs_ref, slots_ref.at[dom, cls], z_send.at[0, hop], z_recv.at[0, hop], target, pl.DeviceIdType.MESH
            )
        )
        z_last.append(
            pltpu.make_async_remote_copy(
                final_ref.at[peer(hop)],
                last_ref.at[:, columns(dom, cls, 1)],
                z_send.at[1, hop],
                z_recv.at[1, hop],
                target,
                pl.DeviceIdType.MESH,
            )
        )
    for move in z_refs + z_last:
        move.start()
    for copy in own:
        copy.wait()

    orders = [list(range(1, bits)) + [0], list(range(bits - 1, 0, -1)) + [0]]

    def begin(stage, piece_of, send_sem, recv_sem):
        moves = []
        for half, order in enumerate(orders):
            target = {"dom": across(order[stage]), "cls": cls}
            for pick in range(1 << stage):
                slot = dom
                for place, old in enumerate(order[:stage]):
                    if pick >> place & 1:
                        slot = slot + (1 << old) - (2 << old) * (lax.div(dom, 1 << old) % 2)
                piece = piece_of(half, slot)
                spot = (1 << stage) - 1 + pick
                moves.append(
                    pltpu.make_async_remote_copy(
                        piece, piece, send_sem(half, spot), recv_sem(half, spot), target, pl.DeviceIdType.MESH
                    )
                )
        for move in moves:
            move.start()
        return moves

    def refs_piece(source):
        rows = half_rows[0]
        return lambda half, slot: slots_ref.at[slot, source, half * rows : (half + 1) * rows]

    def last_piece(half, slot):
        rows = half_rows[1]
        return last_ref.at[half * rows : (half + 1) * rows, columns(slot, 0, groups)]

    sent = z_refs + z_last
    flying = [[]] + [[move] for move in z_refs] + [z_last]
    for stage in range(bits):
        for hop in range(groups + 1):
            for move in flying[hop]:
                move.wait_recv()
            if hop < groups:
                flying[hop] = begin(
                    stage,
                    refs_piece(lax.rem(cls + groups - hop, groups)),
                    lambda half, spot: r_send.at[hop, half, spot],
                    lambda half, spot: r_recv.at[hop, half, spot],
                )
            else:
                flying[hop] = begin(
                    stage,
                    last_piece,
                    lambda half, spot: f_send.at[half, spot],
                    lambda half, spot: f_recv.at[half, spot],
                )
            sent.extend(flying[hop])
    for moves in flying:
        for move in moves:
            move.wait_recv()
    for move in sent:
        move.wait_send()


def score_kernel(parts_ref, refs_ref, out_ref, rolled, total):
    step = pl.program_id(0)
    per_dev = parts_ref.shape[0]
    blocks, names, width = refs_ref.shape
    per_group = names // STEPS
    radii = parts_ref.shape[1] // ANGLES
    for a in range(radii):
        cols = slice(a * ANGLES, (a + 1) * ANGLES)
        image = parts_ref[:, cols]
        for r in range(ROT):
            turned = pltpu.roll(image, r * ASTEP, 1) if r else image
            rolled[r * per_dev : (r + 1) * per_dev, cols] = turned
    product = None
    for b in range(blocks):
        part = lax.dot_general(
            rolled[:, b * width : (b + 1) * width],
            refs_ref[b],
            (((1,), (1,)), ((), ())),
            preferred_element_type=jnp.float32,
        )
        product = part if product is None else product + part

    @pl.when(step == 0)
    def _():
        total[...] = product

    @pl.when(step > 0)
    def _():
        total[...] += product

    @pl.when(step == pl.num_programs(0) - 1)
    def _():
        scale = 1.0 / math.sqrt(RADII * ANGLES)
        pack = 128 // per_group
        for q in range(ROT // pack):
            tiles = [total[(q * pack + j) * per_dev : (q * pack + j + 1) * per_dev, :] * scale for j in range(pack)]
            for s in range(STEPS):
                out_ref[s, :, q * 128 : (q + 1) * 128] = jnp.concatenate(
                    [t[:, s * per_group : (s + 1) * per_group] for t in tiles], axis=1
                )


def per_device(particles, averages, prior_mass, group_ids, class_ids, rot_ids, weights, owners):
    per_dev, pixels = particles.shape
    per_group = averages.shape[0]
    doms, groups = lax.axis_size("dom"), lax.axis_size("cls")
    devices = doms * groups
    width = pixels // devices
    radii = width // ANGLES
    count = per_dev * devices
    classes = per_group * groups

    meta = jnp.stack([group_ids[:, :, 0], class_ids, rot_ids]).astype(jnp.bfloat16)
    meta = jnp.concatenate([meta, weights[None]]).reshape(-1)
    size = meta.shape[0]
    meta = jnp.pad(meta, (0, per_dev * ANGLES - size)).reshape(1, per_dev, ANGLES)
    blocks = particles.reshape(per_dev, devices, radii, ANGLES).transpose(1, 2, 0, 3)
    blocks = blocks.reshape(devices, radii * per_dev, ANGLES)
    blocks = jnp.concatenate([blocks, jnp.broadcast_to(meta, (devices, per_dev, ANGLES))], axis=1)
    band = lax.dynamic_slice_in_dim(averages, lax.axis_index("dom") * groups * width, groups * width, 1)
    band = band.reshape(per_group, groups, width).transpose(1, 0, 2)
    extra = jnp.pad(prior_mass, (0, 8 * width - per_group)).reshape(1, 8, width)
    band = jnp.concatenate([band, jnp.broadcast_to(extra, (groups, 8, width))], axis=1)
    hbm = pl.BlockSpec(memory_space=pl.ANY)
    dma = pltpu.SemaphoreType.DMA
    mine, band = pl.pallas_call(
        functools.partial(exchange_kernel, doms, groups),
        out_shape=(jax.ShapeDtypeStruct(blocks.shape, blocks.dtype), jax.ShapeDtypeStruct(band.shape, band.dtype)),
        in_specs=[hbm, hbm],
        out_specs=(hbm, hbm),
        scratch_shapes=[dma((2,)), dma((devices,)), dma((devices,)), dma((groups,)), dma((groups,))],
        compiler_params=pltpu.CompilerParams(collective_id=1, has_side_effects=True),
        name="exchange",
    )(blocks, band)
    prior = band[:, per_group, :per_group].reshape(classes, 1)

    meta = mine[:, radii * per_dev :, :].reshape(devices, per_dev * ANGLES)[:, :size]
    meta = meta.reshape(devices, 4, STEPS, per_dev).transpose(1, 2, 0, 3).reshape(4, STEPS, count).astype(jnp.float32)
    label = (meta[0] * per_group + meta[1]).astype(jnp.int32)
    shift = (meta[2] * ASTEP).astype(jnp.int32).T

    vmem = pl.BlockSpec(memory_space=pltpu.VMEM)
    refs, final = pl.pallas_call(
        update_kernel,
        out_shape=(
            jax.ShapeDtypeStruct((STEPS * per_group, width), jnp.bfloat16),
            jax.ShapeDtypeStruct((groups, per_group, width), jnp.bfloat16),
        ),
        in_specs=[pl.BlockSpec(memory_space=pltpu.SMEM)] + [vmem] * 6,
        out_specs=(vmem, vmem),
        scratch_shapes=[pltpu.VMEM((classes, width), jnp.float32)],
        compiler_params=pltpu.CompilerParams(vmem_limit_bytes=40 * MIB),
        name="update",
    )(owners, mine, band, label, meta[3], shift, prior)

    all_refs, last = pl.pallas_call(
        functools.partial(gather_kernel, doms, groups),
        out_shape=(
            jax.ShapeDtypeStruct((doms, groups, STEPS * per_group, width), jnp.bfloat16),
            jax.ShapeDtypeStruct((per_group, pixels), jnp.bfloat16),
        ),
        in_specs=[hbm, hbm],
        out_specs=(hbm, hbm),
        scratch_shapes=[
            dma((2,)),
            dma((2, groups)),
            dma((2, groups)),
            dma((groups, 2, doms)),
            dma((groups, 2, doms)),
            dma((2, doms)),
            dma((2, doms)),
        ],
        compiler_params=pltpu.CompilerParams(collective_id=0, has_side_effects=True),
        name="gather",
    )(refs, final)
    all_refs = all_refs.reshape(devices, STEPS * per_group, width)
    last = last.astype(jnp.float32)

    chunks = 8
    scores = pl.pallas_call(
        score_kernel,
        grid=(chunks,),
        out_shape=jax.ShapeDtypeStruct((STEPS, per_dev, ROT * per_group), jnp.float32),
        in_specs=[
            pl.BlockSpec((per_dev, pixels // chunks), lambda c: (0, c)),
            pl.BlockSpec((devices // chunks, STEPS * per_group, width), lambda c: (c, 0, 0)),
        ],
        out_specs=pl.BlockSpec((STEPS, per_dev, ROT * per_group), lambda c: (0, 0, 0)),
        scratch_shapes=[
            pltpu.VMEM((ROT * per_dev, pixels // chunks), jnp.bfloat16),
            pltpu.VMEM((ROT * per_dev, STEPS * per_group), jnp.float32),
        ],
        compiler_params=pltpu.CompilerParams(vmem_limit_bytes=40 * MIB),
        name="scores",
    )(particles, all_refs)
    return scores, last


def solution(mesh):
    return jax.shard_map(
        per_device,
        mesh=mesh,
        in_specs=(
            P(("dom", "cls"), None),
            P("cls", None),
            P("cls"),
            P(None, ("dom", "cls"), None),
            P(None, ("dom", "cls")),
            P(None, ("dom", "cls")),
            P(None, ("dom", "cls")),
            P(),
        ),
        out_specs=(P(None, ("dom", "cls"), None), P("cls", None)),
        check_vma=False,
    )
```

```python
import functools
import math

import jax
import jax.numpy as jnp
from jax import lax
from jax.experimental import pallas as pl
from jax.experimental.pallas import tpu as pltpu
from jax.sharding import PartitionSpec as P

RADII = 128
ANGLES = 128
ROT = 64
STEPS = 4
ASTEP = 2
MIB = 1024 * 1024


def update_kernel(owners_ref, parts_ref, av_ref, refs_ref, last_ref, current):
    senders, rows = parts_ref.shape[:2]
    groups, per_group, wide = av_ref.shape
    width = wide - ANGLES
    radii = width // ANGLES
    per_dev = rows // (radii + 1)
    count, classes = senders * per_dev, groups * per_group
    prior = av_ref[:, :, width:].reshape(classes, ANGLES)
    meta = parts_ref[:, radii * per_dev :, :].reshape(count, ANGLES).astype(jnp.float32)
    lane = lax.broadcasted_iota(jnp.int32, (count, ANGLES), 1)
    class_lane = lax.broadcasted_iota(jnp.int32, (count, classes), 1)
    ones = jnp.ones((count, ANGLES), jnp.bfloat16)
    current[...] = av_ref[:, :, :width].reshape(classes, width)

    def value(kind, step):
        return meta[:, kind * STEPS + step : kind * STEPS + step + 1]

    for step in range(STEPS):
        shift = (value(2, step) * ASTEP).astype(jnp.int32)
        label = (value(0, step) * per_group + value(1, step)).astype(jnp.int32)
        index = (lane - shift) & (ANGLES - 1)
        hot = jnp.where(class_lane == label, value(3, step), 0.0).astype(jnp.bfloat16)

        def summed(values):
            return lax.dot_general(hot, values, (((0,), (0,)), ((), ())), preferred_element_type=jnp.float32)

        inverse = 1.0 / (prior + summed(ones))
        for a in range(radii):
            cols = slice(a * ANGLES, (a + 1) * ANGLES)
            image = parts_ref[:, a * per_dev : (a + 1) * per_dev, :].reshape(count, ANGLES).astype(jnp.float32)
            turned = jnp.take_along_axis(image, index, axis=1).astype(jnp.bfloat16)
            current[:, cols] = (prior * current[:, cols] + summed(turned)) * inverse
        start = pl.multiple_of(owners_ref[step] * per_group, per_group)
        refs_ref[step * per_group : (step + 1) * per_group, :] = current[pl.ds(start, per_group), :].astype(jnp.bfloat16)
    last_ref[...] = current[...].astype(jnp.bfloat16).reshape(groups, per_group, width)


def exchange_kernel(doms, groups, blocks_ref, band_ref, mine_ref, got_ref, own_sem, send, recv, b_send, b_recv):
    dom, cls = lax.axis_index("dom"), lax.axis_index("cls")
    devices = doms * groups
    me = dom * groups + cls

    def peer(hop):
        return lax.rem(me + hop, devices)

    def place(device):
        return {"dom": lax.div(device, groups), "cls": lax.rem(device, groups)}

    barrier = pltpu.get_barrier_semaphore()

    @pl.loop(1, devices)
    def _(hop):
        pl.semaphore_signal(barrier, device_id=place(peer(hop)), device_id_type=pl.DeviceIdType.MESH)

    pl.semaphore_wait(barrier, devices - 1)

    def block(hop):
        return pltpu.make_async_remote_copy(
            blocks_ref.at[peer(hop)],
            mine_ref.at[me],
            send.at[hop],
            recv.at[hop],
            place(peer(hop)),
            pl.DeviceIdType.MESH,
        )

    def band(hop):
        other = lax.rem(cls + hop, groups)
        return pltpu.make_async_remote_copy(
            band_ref.at[other],
            got_ref.at[cls],
            b_send.at[hop],
            b_recv.at[hop],
            {"dom": dom, "cls": other},
            pl.DeviceIdType.MESH,
        )

    @pl.loop(1, devices)
    def _(hop):
        block(hop).start()

    @pl.loop(1, groups)
    def _(hop):
        band(hop).start()

    own = [
        pltpu.make_async_copy(blocks_ref.at[me], mine_ref.at[me], own_sem.at[0]),
        pltpu.make_async_copy(band_ref.at[cls], got_ref.at[cls], own_sem.at[1]),
    ]
    for copy in own:
        copy.start()
    for copy in own:
        copy.wait()

    @pl.loop(1, devices)
    def _(hop):
        block(hop).wait()

    @pl.loop(1, groups)
    def _(hop):
        band(hop).wait()


def gather_kernel(
    doms,
    groups,
    refs_ref,
    final_ref,
    images_ref,
    last_ref,
    scores_ref,
    slots_ref,
    rolled,
    total,
    own_sem,
    z_send,
    z_recv,
    r_send,
    r_recv,
    f_send,
    f_recv,
):
    dom, cls = lax.axis_index("dom"), lax.axis_index("cls")
    bits = doms.bit_length() - 1
    per_group, width = final_ref.shape[1:]

    def across(bit):
        return dom + (1 << bit) - (2 << bit) * (lax.div(dom, 1 << bit) % 2)

    def peer(hop):
        return lax.rem(cls + hop, groups)

    barrier = pltpu.get_barrier_semaphore()
    for hop in range(1, groups):
        pl.semaphore_signal(barrier, device_id={"dom": dom, "cls": peer(hop)}, device_id_type=pl.DeviceIdType.MESH)
    for bit in range(bits):
        pl.semaphore_signal(barrier, device_id={"dom": across(bit), "cls": cls}, device_id_type=pl.DeviceIdType.MESH)
    pl.semaphore_wait(barrier, groups - 1 + bits)

    def columns(which_dom, which_cls, count):
        return pl.ds(pl.multiple_of((which_dom * groups + which_cls) * width, width), count * width)

    half_rows = (refs_ref.shape[0] // 2, per_group // 2)
    own = [
        pltpu.make_async_copy(refs_ref, slots_ref.at[dom, cls], own_sem.at[0]),
        pltpu.make_async_copy(final_ref.at[cls], last_ref.at[:, columns(dom, cls, 1)], own_sem.at[1]),
    ]
    for copy in own:
        copy.start()
    z_refs, z_last = [], []
    for hop in range(1, groups):
        target = {"dom": dom, "cls": peer(hop)}
        z_refs.append(
            pltpu.make_async_remote_copy(
                refs_ref, slots_ref.at[dom, cls], z_send.at[0, hop], z_recv.at[0, hop], target, pl.DeviceIdType.MESH
            )
        )
        z_last.append(
            pltpu.make_async_remote_copy(
                final_ref.at[peer(hop)],
                last_ref.at[:, columns(dom, cls, 1)],
                z_send.at[1, hop],
                z_recv.at[1, hop],
                target,
                pl.DeviceIdType.MESH,
            )
        )
    for move in z_refs + z_last:
        move.start()
    for copy in own:
        copy.wait()

    orders = [list(range(1, bits)) + [0], list(range(bits - 1, 0, -1)) + [0]]

    def begin(stage, piece_of, send_sem, recv_sem):
        moves = []
        for half, order in enumerate(orders):
            target = {"dom": across(order[stage]), "cls": cls}
            for pick in range(1 << stage):
                slot = dom
                for place, old in enumerate(order[:stage]):
                    if pick >> place & 1:
                        slot = slot + (1 << old) - (2 << old) * (lax.div(dom, 1 << old) % 2)
                piece = piece_of(half, slot)
                spot = (1 << stage) - 1 + pick
                moves.append(
                    pltpu.make_async_remote_copy(
                        piece, piece, send_sem(half, spot), recv_sem(half, spot), target, pl.DeviceIdType.MESH
                    )
                )
        for move in moves:
            move.start()
        return moves

    def refs_piece(source):
        rows = half_rows[0]
        return lambda half, slot: slots_ref.at[slot, source, half * rows : (half + 1) * rows]

    def last_piece(half, slot):
        rows = half_rows[1]
        return last_ref.at[half * rows : (half + 1) * rows, columns(slot, 0, groups)]

    radii = width // ANGLES
    per_dev = images_ref.shape[1]
    chunks = 8
    depth = images_ref.shape[0] // chunks

    def roll_chunk(chunk):
        part = slice(chunk * depth, (chunk + 1) * depth)
        images = images_ref[part].reshape(depth * per_dev, ANGLES)
        for r in range(ROT):
            turned = pltpu.roll(images, r * ASTEP, 1) if r else images
            rolled[part, r * per_dev : (r + 1) * per_dev, :] = turned.reshape(depth, per_dev, ANGLES)

    def multiply(source, core):
        @pl.loop(0, doms // 2)
        def _(pair):
            which = 2 * pair + core
            base = (which * groups + source) * radii
            views = jnp.concatenate([rolled[base + j] for j in range(radii)], axis=1)
            total[...] += lax.dot_general(
                views, slots_ref[which, source], (((1,), (1,)), ((), ())), preferred_element_type=jnp.float32
            )

    total[...] = jnp.zeros_like(total)
    todo = list(range(chunks))
    core = lax.rem(dom, 2)
    sent = z_refs + z_last
    flying = [[]] + [[move] for move in z_refs] + [z_last]
    for stage in range(bits):
        for hop in range(groups + 1):
            for move in flying[hop]:
                move.wait_recv()
            if hop < groups:
                source = lax.rem(cls + groups - hop, groups)
                flying[hop] = begin(
                    stage,
                    refs_piece(source),
                    lambda half, spot: r_send.at[hop, half, spot],
                    lambda half, spot: r_recv.at[hop, half, spot],
                )
            else:
                flying[hop] = begin(
                    stage,
                    last_piece,
                    lambda half, spot: f_send.at[half, spot],
                    lambda half, spot: f_recv.at[half, spot],
                )
            sent.extend(flying[hop])
            if stage == bits - 1:
                for chunk in todo:
                    roll_chunk(chunk)
                todo = []
                if hop < groups:
                    multiply(source, core)
            elif hop < groups:
                for chunk in todo[: 2 if stage == hop == 0 else 1]:
                    roll_chunk(chunk)
                todo = todo[2 if stage == hop == 0 else 1 :]
    for hop in range(groups + 1):
        for move in flying[hop]:
            move.wait_recv()
        if hop < groups:
            multiply(lax.rem(cls + groups - hop, groups), 1 - core)

    scale = 1.0 / math.sqrt(RADII * ANGLES)
    pack = ANGLES // per_group
    for q in range(ROT // pack):
        tiles = [total[(q * pack + j) * per_dev : (q * pack + j + 1) * per_dev, :] * scale for j in range(pack)]
        for s in range(STEPS):
            scores_ref[s, :, q * ANGLES : (q + 1) * ANGLES] = jnp.concatenate(
                [t[:, s * per_group : (s + 1) * per_group] for t in tiles], axis=1
            )
    for move in sent:
        move.wait_send()


def per_device(particles, averages, prior_mass, group_ids, class_ids, rot_ids, weights, owners):
    per_dev, pixels = particles.shape
    per_group = averages.shape[0]
    doms, groups = lax.axis_size("dom"), lax.axis_size("cls")
    devices = doms * groups
    width = pixels // devices
    radii = width // ANGLES
    classes = per_group * groups

    meta = jnp.stack([group_ids[:, :, 0], class_ids, rot_ids]).astype(jnp.bfloat16)
    meta = jnp.concatenate([meta, weights[None]]).reshape(4 * STEPS, per_dev).T
    meta = jnp.pad(meta, ((0, 0), (0, ANGLES - 4 * STEPS)))[None]
    images = particles.reshape(per_dev, pixels // ANGLES, ANGLES).transpose(1, 0, 2)
    blocks = images.reshape(devices, radii * per_dev, ANGLES)
    blocks = jnp.concatenate([blocks, jnp.broadcast_to(meta, (devices, per_dev, ANGLES))], axis=1)
    band = lax.dynamic_slice_in_dim(averages, lax.axis_index("dom") * groups * width, groups * width, 1)
    band = band.reshape(per_group, groups, width).transpose(1, 0, 2)
    extra = jnp.broadcast_to(prior_mass[None, :, None], (groups, per_group, ANGLES))
    band = jnp.concatenate([band, extra], axis=2)
    hbm = pl.BlockSpec(memory_space=pl.ANY)
    dma = pltpu.SemaphoreType.DMA
    mine, band = pl.pallas_call(
        functools.partial(exchange_kernel, doms, groups),
        out_shape=(jax.ShapeDtypeStruct(blocks.shape, blocks.dtype), jax.ShapeDtypeStruct(band.shape, band.dtype)),
        in_specs=[hbm, hbm],
        out_specs=(hbm, hbm),
        scratch_shapes=[dma((2,)), dma((devices,)), dma((devices,)), dma((groups,)), dma((groups,))],
        compiler_params=pltpu.CompilerParams(collective_id=1, has_side_effects=True),
        name="exchange",
    )(blocks, band)
    vmem = pl.BlockSpec(memory_space=pltpu.VMEM)
    refs, final = pl.pallas_call(
        update_kernel,
        out_shape=(
            jax.ShapeDtypeStruct((STEPS * per_group, width), jnp.bfloat16),
            jax.ShapeDtypeStruct((groups, per_group, width), jnp.bfloat16),
        ),
        in_specs=[pl.BlockSpec(memory_space=pltpu.SMEM)] + [vmem] * 2,
        out_specs=(vmem, vmem),
        scratch_shapes=[pltpu.VMEM((classes, width), jnp.float32)],
        compiler_params=pltpu.CompilerParams(vmem_limit_bytes=40 * MIB),
        name="update",
    )(owners, mine, band)

    last, scores = pl.pallas_call(
        functools.partial(gather_kernel, doms, groups),
        out_shape=(
            jax.ShapeDtypeStruct((per_group, pixels), jnp.bfloat16),
            jax.ShapeDtypeStruct((STEPS, per_dev, ROT * per_group), jnp.float32),
        ),
        in_specs=[hbm, hbm, vmem],
        out_specs=(hbm, vmem),
        scratch_shapes=[
            pltpu.VMEM((doms, groups, STEPS * per_group, width), jnp.bfloat16),
            pltpu.VMEM((pixels // ANGLES, ROT * per_dev, ANGLES), jnp.bfloat16),
            pltpu.VMEM((ROT * per_dev, STEPS * per_group), jnp.float32),
            dma((2,)),
            dma((2, groups)),
            dma((2, groups)),
            dma((groups, 2, doms)),
            dma((groups, 2, doms)),
            dma((2, doms)),
            dma((2, doms)),
        ],
        compiler_params=pltpu.CompilerParams(
            collective_id=0, has_side_effects=True, vmem_limit_bytes=52 * MIB
        ),
        name="gather_scores",
    )(refs, final, images)
    return scores, last.astype(jnp.float32)


def solution(mesh):
    return jax.shard_map(
        per_device,
        mesh=mesh,
        in_specs=(
            P(("dom", "cls"), None),
            P("cls", None),
            P("cls"),
            P(None, ("dom", "cls"), None),
            P(None, ("dom", "cls")),
            P(None, ("dom", "cls")),
            P(None, ("dom", "cls")),
            P(),
        ),
        out_specs=(P(None, ("dom", "cls"), None), P("cls", None)),
        check_vma=False,
    )
```

```python
import functools
import math

import jax
import jax.numpy as jnp
from jax import lax
from jax.experimental import pallas as pl
from jax.experimental.pallas import tpu as pltpu
from jax.sharding import PartitionSpec as P

RADII = 128
ANGLES = 128
ROT = 64
STEPS = 4
ASTEP = 2
MIB = 1024 * 1024


def update_kernel(owners_ref, parts_ref, av_ref, refs_ref, last_ref, current):
    senders, rows = parts_ref.shape[:2]
    groups, per_group, wide = av_ref.shape
    width = wide - ANGLES
    radii = width // ANGLES
    per_dev = rows // (radii + 1)
    count, classes = senders * per_dev, groups * per_group
    prior = av_ref[:, :, width:].reshape(classes, ANGLES)
    meta = parts_ref[:, radii * per_dev :, :].reshape(count, ANGLES).astype(jnp.float32)
    lane = lax.broadcasted_iota(jnp.int32, (count, ANGLES), 1)
    class_lane = lax.broadcasted_iota(jnp.int32, (count, classes), 1)
    ones = jnp.ones((count, ANGLES), jnp.bfloat16)
    current[...] = av_ref[:, :, :width].reshape(classes, width)

    def value(kind, step):
        return meta[:, kind * STEPS + step : kind * STEPS + step + 1]

    for step in range(STEPS):
        shift = (value(2, step) * ASTEP).astype(jnp.int32)
        label = (value(0, step) * per_group + value(1, step)).astype(jnp.int32)
        index = (lane - shift) & (ANGLES - 1)
        hot = jnp.where(class_lane == label, value(3, step), 0.0).astype(jnp.bfloat16)

        def summed(values):
            return lax.dot_general(hot, values, (((0,), (0,)), ((), ())), preferred_element_type=jnp.float32)

        inverse = 1.0 / (prior + summed(ones))
        for a in range(radii):
            cols = slice(a * ANGLES, (a + 1) * ANGLES)
            image = parts_ref[:, a * per_dev : (a + 1) * per_dev, :].reshape(count, ANGLES).astype(jnp.float32)
            turned = jnp.take_along_axis(image, index, axis=1).astype(jnp.bfloat16)
            current[:, cols] = (prior * current[:, cols] + summed(turned)) * inverse
        start = pl.multiple_of(owners_ref[step] * per_group, per_group)
        refs_ref[step * per_group : (step + 1) * per_group, :] = current[pl.ds(start, per_group), :].astype(jnp.bfloat16)
    last_ref[...] = current[...].astype(jnp.bfloat16).reshape(groups, per_group, width)


def exchange_kernel(doms, groups, blocks_ref, band_ref, mine_ref, got_ref, own_sem, send, recv, b_send, b_recv):
    dom, cls = lax.axis_index("dom"), lax.axis_index("cls")
    devices = doms * groups
    me = dom * groups + cls

    def peer(hop):
        return lax.rem(me + hop, devices)

    def place(device):
        return {"dom": lax.div(device, groups), "cls": lax.rem(device, groups)}

    barrier = pltpu.get_barrier_semaphore()

    @pl.loop(1, devices)
    def _(hop):
        pl.semaphore_signal(barrier, device_id=place(peer(hop)), device_id_type=pl.DeviceIdType.MESH)

    pl.semaphore_wait(barrier, devices - 1)

    def block(hop):
        return pltpu.make_async_remote_copy(
            blocks_ref.at[peer(hop)],
            mine_ref.at[me],
            send.at[hop],
            recv.at[hop],
            place(peer(hop)),
            pl.DeviceIdType.MESH,
        )

    def band(hop):
        other = lax.rem(cls + hop, groups)
        return pltpu.make_async_remote_copy(
            band_ref.at[other],
            got_ref.at[cls],
            b_send.at[hop],
            b_recv.at[hop],
            {"dom": dom, "cls": other},
            pl.DeviceIdType.MESH,
        )

    @pl.loop(1, devices)
    def _(hop):
        block(hop).start()

    @pl.loop(1, groups)
    def _(hop):
        band(hop).start()

    own = [
        pltpu.make_async_copy(blocks_ref.at[me], mine_ref.at[me], own_sem.at[0]),
        pltpu.make_async_copy(band_ref.at[cls], got_ref.at[cls], own_sem.at[1]),
    ]
    for copy in own:
        copy.start()
    for copy in own:
        copy.wait()

    @pl.loop(1, devices)
    def _(hop):
        block(hop).wait()

    @pl.loop(1, groups)
    def _(hop):
        band(hop).wait()


def gather_kernel(
    doms,
    groups,
    refs_ref,
    final_ref,
    images_ref,
    last_ref,
    scores_ref,
    slots_ref,
    rolled,
    total,
    own_sem,
    z_send,
    z_recv,
    r_send,
    r_recv,
    f_send,
    f_recv,
):
    dom, cls = lax.axis_index("dom"), lax.axis_index("cls")
    bits = doms.bit_length() - 1
    per_group, width = final_ref.shape[1:]

    def across(bit):
        return dom + (1 << bit) - (2 << bit) * (lax.div(dom, 1 << bit) % 2)

    def peer(hop):
        return lax.rem(cls + hop, groups)

    barrier = pltpu.get_barrier_semaphore()
    for hop in range(1, groups):
        pl.semaphore_signal(barrier, device_id={"dom": dom, "cls": peer(hop)}, device_id_type=pl.DeviceIdType.MESH)
    for bit in range(bits):
        pl.semaphore_signal(barrier, device_id={"dom": across(bit), "cls": cls}, device_id_type=pl.DeviceIdType.MESH)
    pl.semaphore_wait(barrier, groups - 1 + bits)

    def columns(which_dom, which_cls, count):
        return pl.ds(pl.multiple_of((which_dom * groups + which_cls) * width, width), count * width)

    half_rows = (refs_ref.shape[0] // 2, per_group // 2)
    own = [
        pltpu.make_async_copy(refs_ref, slots_ref.at[dom, cls], own_sem.at[0]),
        pltpu.make_async_copy(final_ref.at[cls], last_ref.at[:, columns(dom, cls, 1)], own_sem.at[1]),
    ]
    for copy in own:
        copy.start()
    z_refs, z_last = [], []
    for hop in range(1, groups):
        target = {"dom": dom, "cls": peer(hop)}
        z_refs.append(
            pltpu.make_async_remote_copy(
                refs_ref, slots_ref.at[dom, cls], z_send.at[0, hop], z_recv.at[0, hop], target, pl.DeviceIdType.MESH
            )
        )
        z_last.append(
            pltpu.make_async_remote_copy(
                final_ref.at[peer(hop)],
                last_ref.at[:, columns(dom, cls, 1)],
                z_send.at[1, hop],
                z_recv.at[1, hop],
                target,
                pl.DeviceIdType.MESH,
            )
        )
    for move in z_refs + z_last:
        move.start()
    for copy in own:
        copy.wait()

    orders = [list(range(1, bits)) + [0], list(range(bits - 1, 0, -1)) + [0]]

    def begin(stage, piece_of, send_sem, recv_sem):
        moves = []
        for half, order in enumerate(orders):
            target = {"dom": across(order[stage]), "cls": cls}
            for pick in range(1 << stage):
                slot = dom
                for place, old in enumerate(order[:stage]):
                    if pick >> place & 1:
                        slot = slot + (1 << old) - (2 << old) * (lax.div(dom, 1 << old) % 2)
                piece = piece_of(half, slot)
                spot = (1 << stage) - 1 + pick
                moves.append(
                    pltpu.make_async_remote_copy(
                        piece, piece, send_sem(half, spot), recv_sem(half, spot), target, pl.DeviceIdType.MESH
                    )
                )
        for move in moves:
            move.start()
        return moves

    def refs_piece(source):
        rows = half_rows[0]
        return lambda half, slot: slots_ref.at[slot, source, half * rows : (half + 1) * rows]

    def last_piece(half, slot):
        rows = half_rows[1]
        return last_ref.at[half * rows : (half + 1) * rows, columns(slot, 0, groups)]

    radii = width // ANGLES
    per_dev = images_ref.shape[1]
    chunks = 8
    depth = images_ref.shape[0] // chunks

    def roll_chunk(chunk):
        part = slice(chunk * depth, (chunk + 1) * depth)
        images = images_ref[part].reshape(depth * per_dev, ANGLES)
        for r in range(ROT):
            turned = pltpu.roll(images, r * ASTEP, 1) if r else images
            rolled[part, r * per_dev : (r + 1) * per_dev, :] = turned.reshape(depth, per_dev, ANGLES)

    def multiply(source, core):
        @pl.loop(0, doms // 2)
        def _(pair):
            which = 2 * pair + core
            base = (which * groups + source) * radii
            views = jnp.concatenate([rolled[base + j] for j in range(radii)], axis=1)
            total[...] += lax.dot_general(
                views, slots_ref[which, source], (((1,), (1,)), ((), ())), preferred_element_type=jnp.float32
            )

    total[...] = jnp.zeros_like(total)
    todo = list(range(chunks))
    core = lax.rem(dom, 2)
    sent = z_refs + z_last
    flying = [[]] + [[move] for move in z_refs] + [z_last]
    for tick in range(groups + bits):
        for stage in reversed(range(bits)):
            hop = tick - stage
            if hop < 0 or hop > groups:
                continue
            for move in flying[hop]:
                move.wait_recv()
            if hop < groups:
                flying[hop] = begin(
                    stage,
                    refs_piece(lax.rem(cls + groups - hop, groups)),
                    lambda half, spot: r_send.at[hop, half, spot],
                    lambda half, spot: r_recv.at[hop, half, spot],
                )
            else:
                flying[hop] = begin(
                    stage,
                    last_piece,
                    lambda half, spot: f_send.at[half, spot],
                    lambda half, spot: f_recv.at[half, spot],
                )
            sent.extend(flying[hop])
        for chunk in todo[:3]:
            roll_chunk(chunk)
        todo = todo[3:]
        landed = tick - bits + 1
        if 0 <= landed < groups:
            multiply(lax.rem(cls + groups - landed, groups), core)
        if 1 <= landed <= groups:
            for move in flying[landed - 1]:
                move.wait_recv()
            multiply(lax.rem(cls + groups - landed + 1, groups), 1 - core)
    for move in flying[groups]:
        move.wait_recv()

    scale = 1.0 / math.sqrt(RADII * ANGLES)
    pack = ANGLES // per_group
    for q in range(ROT // pack):
        tiles = [total[(q * pack + j) * per_dev : (q * pack + j + 1) * per_dev, :] * scale for j in range(pack)]
        for s in range(STEPS):
            scores_ref[s, :, q * ANGLES : (q + 1) * ANGLES] = jnp.concatenate(
                [t[:, s * per_group : (s + 1) * per_group] for t in tiles], axis=1
            )
    for move in sent:
        move.wait_send()


def per_device(particles, averages, prior_mass, group_ids, class_ids, rot_ids, weights, owners):
    per_dev, pixels = particles.shape
    per_group = averages.shape[0]
    doms, groups = lax.axis_size("dom"), lax.axis_size("cls")
    devices = doms * groups
    width = pixels // devices
    radii = width // ANGLES
    classes = per_group * groups

    meta = jnp.stack([group_ids[:, :, 0], class_ids, rot_ids]).astype(jnp.bfloat16)
    meta = jnp.concatenate([meta, weights[None]]).reshape(4 * STEPS, per_dev).T
    meta = jnp.pad(meta, ((0, 0), (0, ANGLES - 4 * STEPS)))[None]
    images = particles.reshape(per_dev, pixels // ANGLES, ANGLES).transpose(1, 0, 2)
    blocks = images.reshape(devices, radii * per_dev, ANGLES)
    blocks = jnp.concatenate([blocks, jnp.broadcast_to(meta, (devices, per_dev, ANGLES))], axis=1)
    band = lax.dynamic_slice_in_dim(averages, lax.axis_index("dom") * groups * width, groups * width, 1)
    band = band.reshape(per_group, groups, width).transpose(1, 0, 2)
    extra = jnp.broadcast_to(prior_mass[None, :, None], (groups, per_group, ANGLES))
    band = jnp.concatenate([band, extra], axis=2)
    hbm = pl.BlockSpec(memory_space=pl.ANY)
    dma = pltpu.SemaphoreType.DMA
    mine, band = pl.pallas_call(
        functools.partial(exchange_kernel, doms, groups),
        out_shape=(jax.ShapeDtypeStruct(blocks.shape, blocks.dtype), jax.ShapeDtypeStruct(band.shape, band.dtype)),
        in_specs=[hbm, hbm],
        out_specs=(hbm, hbm),
        scratch_shapes=[dma((2,)), dma((devices,)), dma((devices,)), dma((groups,)), dma((groups,))],
        compiler_params=pltpu.CompilerParams(collective_id=1, has_side_effects=True),
        name="exchange",
    )(blocks, band)
    vmem = pl.BlockSpec(memory_space=pltpu.VMEM)
    refs, final = pl.pallas_call(
        update_kernel,
        out_shape=(
            jax.ShapeDtypeStruct((STEPS * per_group, width), jnp.bfloat16),
            jax.ShapeDtypeStruct((groups, per_group, width), jnp.bfloat16),
        ),
        in_specs=[pl.BlockSpec(memory_space=pltpu.SMEM)] + [vmem] * 2,
        out_specs=(vmem, vmem),
        scratch_shapes=[pltpu.VMEM((classes, width), jnp.float32)],
        compiler_params=pltpu.CompilerParams(vmem_limit_bytes=40 * MIB),
        name="update",
    )(owners, mine, band)

    last, scores = pl.pallas_call(
        functools.partial(gather_kernel, doms, groups),
        out_shape=(
            jax.ShapeDtypeStruct((per_group, pixels), jnp.bfloat16),
            jax.ShapeDtypeStruct((STEPS, per_dev, ROT * per_group), jnp.float32),
        ),
        in_specs=[hbm, hbm, vmem],
        out_specs=(hbm, vmem),
        scratch_shapes=[
            pltpu.VMEM((doms, groups, STEPS * per_group, width), jnp.bfloat16),
            pltpu.VMEM((pixels // ANGLES, ROT * per_dev, ANGLES), jnp.bfloat16),
            pltpu.VMEM((ROT * per_dev, STEPS * per_group), jnp.float32),
            dma((2,)),
            dma((2, groups)),
            dma((2, groups)),
            dma((groups, 2, doms)),
            dma((groups, 2, doms)),
            dma((2, doms)),
            dma((2, doms)),
        ],
        compiler_params=pltpu.CompilerParams(
            collective_id=0, has_side_effects=True, vmem_limit_bytes=52 * MIB
        ),
        name="gather_scores",
    )(refs, final, images)
    return scores, last.astype(jnp.float32)


def solution(mesh):
    return jax.shard_map(
        per_device,
        mesh=mesh,
        in_specs=(
            P(("dom", "cls"), None),
            P("cls", None),
            P("cls"),
            P(None, ("dom", "cls"), None),
            P(None, ("dom", "cls")),
            P(None, ("dom", "cls")),
            P(None, ("dom", "cls")),
            P(),
        ),
        out_specs=(P(None, ("dom", "cls"), None), P("cls", None)),
        check_vma=False,
    )
```

```python
import functools
import math

import jax
import jax.numpy as jnp
from jax import lax
from jax.experimental import pallas as pl
from jax.experimental.pallas import tpu as pltpu
from jax.sharding import PartitionSpec as P

RADII = 128
ANGLES = 128
ROT = 64
STEPS = 4
ASTEP = 2
MIB = 1024 * 1024


def update_kernel(owners_ref, parts_ref, av_ref, refs_ref, last_ref, current):
    senders, rows = parts_ref.shape[:2]
    groups, per_group, wide = av_ref.shape
    width = wide - ANGLES
    radii = width // ANGLES
    per_dev = rows // (radii + 1)
    count, classes = senders * per_dev, groups * per_group
    prior = av_ref[:, :, width:].reshape(classes, ANGLES)
    meta = parts_ref[:, radii * per_dev :, :].reshape(count, ANGLES).astype(jnp.float32)
    lane = lax.broadcasted_iota(jnp.int32, (count, ANGLES), 1)
    class_lane = lax.broadcasted_iota(jnp.int32, (count, classes), 1)
    ones = jnp.ones((count, ANGLES), jnp.bfloat16)
    current[...] = av_ref[:, :, :width].reshape(classes, width)

    def value(kind, step):
        return meta[:, kind * STEPS + step : kind * STEPS + step + 1]

    for step in range(STEPS):
        shift = (value(2, step) * ASTEP).astype(jnp.int32)
        label = (value(0, step) * per_group + value(1, step)).astype(jnp.int32)
        index = (lane - shift) & (ANGLES - 1)
        hot = jnp.where(class_lane == label, value(3, step), 0.0).astype(jnp.bfloat16)

        def summed(values):
            return lax.dot_general(hot, values, (((0,), (0,)), ((), ())), preferred_element_type=jnp.float32)

        inverse = 1.0 / (prior + summed(ones))
        for a in range(radii):
            cols = slice(a * ANGLES, (a + 1) * ANGLES)
            image = parts_ref[:, a * per_dev : (a + 1) * per_dev, :].reshape(count, ANGLES).astype(jnp.float32)
            turned = jnp.take_along_axis(image, index, axis=1).astype(jnp.bfloat16)
            current[:, cols] = (prior * current[:, cols] + summed(turned)) * inverse
        start = pl.multiple_of(owners_ref[step] * per_group, per_group)
        refs_ref[step * per_group : (step + 1) * per_group, :] = current[pl.ds(start, per_group), :].astype(jnp.bfloat16)
    last_ref[...] = current[...].astype(jnp.bfloat16).reshape(groups, per_group, width)


def exchange_kernel(doms, groups, blocks_ref, band_ref, mine_ref, got_ref, own_sem, send, recv, b_send, b_recv):
    dom, cls = lax.axis_index("dom"), lax.axis_index("cls")
    devices = doms * groups
    me = dom * groups + cls

    def peer(hop):
        return lax.rem(me + hop, devices)

    def place(device):
        return {"dom": lax.div(device, groups), "cls": lax.rem(device, groups)}

    barrier = pltpu.get_barrier_semaphore()

    @pl.loop(1, devices)
    def _(hop):
        pl.semaphore_signal(barrier, device_id=place(peer(hop)), device_id_type=pl.DeviceIdType.MESH)

    pl.semaphore_wait(barrier, devices - 1)

    def block(hop):
        return pltpu.make_async_remote_copy(
            blocks_ref.at[peer(hop)],
            mine_ref.at[me],
            send.at[hop],
            recv.at[hop],
            place(peer(hop)),
            pl.DeviceIdType.MESH,
        )

    def band(hop):
        other = lax.rem(cls + hop, groups)
        return pltpu.make_async_remote_copy(
            band_ref.at[other],
            got_ref.at[cls],
            b_send.at[hop],
            b_recv.at[hop],
            {"dom": dom, "cls": other},
            pl.DeviceIdType.MESH,
        )

    @pl.loop(1, groups)
    def _(hop):
        band(hop).start()

    @pl.loop(1, devices)
    def _(hop):
        block(hop).start()

    own = [
        pltpu.make_async_copy(blocks_ref.at[me], mine_ref.at[me], own_sem.at[0]),
        pltpu.make_async_copy(band_ref.at[cls], got_ref.at[cls], own_sem.at[1]),
    ]
    for copy in own:
        copy.start()
    for copy in own:
        copy.wait()

    @pl.loop(1, devices)
    def _(hop):
        block(hop).wait()

    @pl.loop(1, groups)
    def _(hop):
        band(hop).wait()


def gather_kernel(
    doms,
    groups,
    refs_ref,
    final_ref,
    images_ref,
    last_ref,
    scores_ref,
    slots_ref,
    rolled,
    total,
    own_sem,
    z_send,
    z_recv,
    r_send,
    r_recv,
    f_send,
    f_recv,
):
    dom, cls = lax.axis_index("dom"), lax.axis_index("cls")
    bits = doms.bit_length() - 1
    per_group, width = final_ref.shape[1:]

    def across(bit):
        return dom + (1 << bit) - (2 << bit) * (lax.div(dom, 1 << bit) % 2)

    def peer(hop):
        return lax.rem(cls + hop, groups)

    barrier = pltpu.get_barrier_semaphore()
    for hop in range(1, groups):
        pl.semaphore_signal(barrier, device_id={"dom": dom, "cls": peer(hop)}, device_id_type=pl.DeviceIdType.MESH)
    for bit in range(bits):
        pl.semaphore_signal(barrier, device_id={"dom": across(bit), "cls": cls}, device_id_type=pl.DeviceIdType.MESH)
    pl.semaphore_wait(barrier, groups - 1 + bits)

    def columns(which_dom, which_cls, count):
        return pl.ds(pl.multiple_of((which_dom * groups + which_cls) * width, width), count * width)

    half_rows = (refs_ref.shape[0] // 2, per_group // 2)
    own = [
        pltpu.make_async_copy(refs_ref, slots_ref.at[dom, cls], own_sem.at[0]),
        pltpu.make_async_copy(final_ref.at[cls], last_ref.at[:, columns(dom, cls, 1)], own_sem.at[1]),
    ]
    for copy in own:
        copy.start()
    z_refs, z_last = [], []
    for hop in range(1, groups):
        target = {"dom": dom, "cls": peer(hop)}
        z_refs.append(
            pltpu.make_async_remote_copy(
                refs_ref, slots_ref.at[dom, cls], z_send.at[0, hop], z_recv.at[0, hop], target, pl.DeviceIdType.MESH
            )
        )
        z_last.append(
            pltpu.make_async_remote_copy(
                final_ref.at[peer(hop)],
                last_ref.at[:, columns(dom, cls, 1)],
                z_send.at[1, hop],
                z_recv.at[1, hop],
                target,
                pl.DeviceIdType.MESH,
            )
        )
    for move in z_refs + z_last:
        move.start()
    for copy in own:
        copy.wait()

    orders = [list(range(1, bits)) + [0], list(range(bits - 1, 0, -1)) + [0]]

    def begin(stage, piece_of, send_sem, recv_sem):
        moves = []
        for half, order in enumerate(orders):
            target = {"dom": across(order[stage]), "cls": cls}
            for pick in range(1 << stage):
                slot = dom
                for place, old in enumerate(order[:stage]):
                    if pick >> place & 1:
                        slot = slot + (1 << old) - (2 << old) * (lax.div(dom, 1 << old) % 2)
                piece = piece_of(half, slot)
                spot = (1 << stage) - 1 + pick
                moves.append(
                    pltpu.make_async_remote_copy(
                        piece, piece, send_sem(half, spot), recv_sem(half, spot), target, pl.DeviceIdType.MESH
                    )
                )
        for move in moves:
            move.start()
        return moves

    def refs_piece(source):
        rows = half_rows[0]
        return lambda half, slot: slots_ref.at[slot, source, half * rows : (half + 1) * rows]

    def last_piece(half, slot):
        rows = half_rows[1]
        return last_ref.at[half * rows : (half + 1) * rows, columns(slot, 0, groups)]

    radii = width // ANGLES
    per_dev = images_ref.shape[1]
    chunks = 8
    depth = images_ref.shape[0] // chunks

    def roll_chunk(chunk):
        part = slice(chunk * depth, (chunk + 1) * depth)
        images = images_ref[part].reshape(depth * per_dev, ANGLES)
        for r in range(ROT):
            turned = pltpu.roll(images, r * ASTEP, 1) if r else images
            rolled[part, r * per_dev : (r + 1) * per_dev, :] = turned.reshape(depth, per_dev, ANGLES)

    def multiply(source, core):
        @pl.loop(0, doms // 2)
        def _(pair):
            which = 2 * pair + core
            base = (which * groups + source) * radii
            views = jnp.concatenate([rolled[base + j] for j in range(radii)], axis=1)
            total[...] += lax.dot_general(
                views, slots_ref[which, source], (((1,), (1,)), ((), ())), preferred_element_type=jnp.float32
            )

    total[...] = jnp.zeros_like(total)
    todo = list(range(chunks))
    core = lax.rem(dom, 2)
    sent = z_refs + z_last
    flying = [[]] + [[move] for move in z_refs] + [z_last]
    for tick in range(groups + bits):
        for stage in reversed(range(bits)):
            hop = tick - stage
            if hop < 0 or hop > groups:
                continue
            for move in flying[hop]:
                move.wait_recv()
            if hop < groups:
                flying[hop] = begin(
                    stage,
                    refs_piece(lax.rem(cls + groups - hop, groups)),
                    lambda half, spot: r_send.at[hop, half, spot],
                    lambda half, spot: r_recv.at[hop, half, spot],
                )
            else:
                flying[hop] = begin(
                    stage,
                    last_piece,
                    lambda half, spot: f_send.at[half, spot],
                    lambda half, spot: f_recv.at[half, spot],
                )
            sent.extend(flying[hop])
        for chunk in todo[:3]:
            roll_chunk(chunk)
        todo = todo[3:]
        landed = tick - bits + 1
        if 0 <= landed < groups:
            multiply(lax.rem(cls + groups - landed, groups), core)
        if 1 <= landed <= groups:
            for move in flying[landed - 1]:
                move.wait_recv()
            multiply(lax.rem(cls + groups - landed + 1, groups), 1 - core)
    for move in flying[groups]:
        move.wait_recv()

    scale = 1.0 / math.sqrt(RADII * ANGLES)
    pack = ANGLES // per_group
    for q in range(ROT // pack):
        tiles = [total[(q * pack + j) * per_dev : (q * pack + j + 1) * per_dev, :] * scale for j in range(pack)]
        for s in range(STEPS):
            scores_ref[s, :, q * ANGLES : (q + 1) * ANGLES] = jnp.concatenate(
                [t[:, s * per_group : (s + 1) * per_group] for t in tiles], axis=1
            )
    for move in sent:
        move.wait_send()


def per_device(particles, averages, prior_mass, group_ids, class_ids, rot_ids, weights, owners):
    per_dev, pixels = particles.shape
    per_group = averages.shape[0]
    doms, groups = lax.axis_size("dom"), lax.axis_size("cls")
    devices = doms * groups
    width = pixels // devices
    radii = width // ANGLES
    classes = per_group * groups

    meta = jnp.stack([group_ids[:, :, 0], class_ids, rot_ids]).astype(jnp.bfloat16)
    meta = jnp.concatenate([meta, weights[None]]).reshape(4 * STEPS, per_dev).T
    meta = jnp.pad(meta, ((0, 0), (0, ANGLES - 4 * STEPS)))[None]
    images = particles.reshape(per_dev, pixels // ANGLES, ANGLES).transpose(1, 0, 2)
    blocks = images.reshape(devices, radii * per_dev, ANGLES)
    blocks = jnp.concatenate([blocks, jnp.broadcast_to(meta, (devices, per_dev, ANGLES))], axis=1)
    band = lax.dynamic_slice_in_dim(averages, lax.axis_index("dom") * groups * width, groups * width, 1)
    band = band.reshape(per_group, groups, width).transpose(1, 0, 2)
    extra = jnp.broadcast_to(prior_mass[None, :, None], (groups, per_group, ANGLES))
    band = jnp.concatenate([band, extra], axis=2)
    hbm = pl.BlockSpec(memory_space=pl.ANY)
    dma = pltpu.SemaphoreType.DMA
    mine, band = pl.pallas_call(
        functools.partial(exchange_kernel, doms, groups),
        out_shape=(jax.ShapeDtypeStruct(blocks.shape, blocks.dtype), jax.ShapeDtypeStruct(band.shape, band.dtype)),
        in_specs=[hbm, hbm],
        out_specs=(hbm, hbm),
        scratch_shapes=[dma((2,)), dma((devices,)), dma((devices,)), dma((groups,)), dma((groups,))],
        compiler_params=pltpu.CompilerParams(collective_id=1, has_side_effects=True),
        name="exchange",
    )(blocks, band)
    vmem = pl.BlockSpec(memory_space=pltpu.VMEM)
    refs, final = pl.pallas_call(
        update_kernel,
        out_shape=(
            jax.ShapeDtypeStruct((STEPS * per_group, width), jnp.bfloat16),
            jax.ShapeDtypeStruct((groups, per_group, width), jnp.bfloat16),
        ),
        in_specs=[pl.BlockSpec(memory_space=pltpu.SMEM)] + [vmem] * 2,
        out_specs=(vmem, vmem),
        scratch_shapes=[pltpu.VMEM((classes, width), jnp.float32)],
        compiler_params=pltpu.CompilerParams(vmem_limit_bytes=40 * MIB),
        name="update",
    )(owners, mine, band)

    last, scores = pl.pallas_call(
        functools.partial(gather_kernel, doms, groups),
        out_shape=(
            jax.ShapeDtypeStruct((per_group, pixels), jnp.bfloat16),
            jax.ShapeDtypeStruct((STEPS, per_dev, ROT * per_group), jnp.float32),
        ),
        in_specs=[hbm, hbm, vmem],
        out_specs=(hbm, vmem),
        scratch_shapes=[
            pltpu.VMEM((doms, groups, STEPS * per_group, width), jnp.bfloat16),
            pltpu.VMEM((pixels // ANGLES, ROT * per_dev, ANGLES), jnp.bfloat16),
            pltpu.VMEM((ROT * per_dev, STEPS * per_group), jnp.float32),
            dma((2,)),
            dma((2, groups)),
            dma((2, groups)),
            dma((groups, 2, doms)),
            dma((groups, 2, doms)),
            dma((2, doms)),
            dma((2, doms)),
        ],
        compiler_params=pltpu.CompilerParams(
            collective_id=0, has_side_effects=True, vmem_limit_bytes=52 * MIB
        ),
        name="gather_scores",
    )(refs, final, images)
    return scores, last.astype(jnp.float32)


def solution(mesh):
    return jax.shard_map(
        per_device,
        mesh=mesh,
        in_specs=(
            P(("dom", "cls"), None),
            P("cls", None),
            P("cls"),
            P(None, ("dom", "cls"), None),
            P(None, ("dom", "cls")),
            P(None, ("dom", "cls")),
            P(None, ("dom", "cls")),
            P(),
        ),
        out_specs=(P(None, ("dom", "cls"), None), P("cls", None)),
        check_vma=False,
    )
```

```python
import functools
import math

import jax
import jax.numpy as jnp
from jax import lax
from jax.experimental import pallas as pl
from jax.experimental.pallas import tpu as pltpu
from jax.sharding import PartitionSpec as P

RADII = 128
ANGLES = 128
ROT = 64
STEPS = 4
ASTEP = 2
MIB = 1024 * 1024


def update_kernel(owners_ref, parts_ref, av_ref, refs_ref, last_ref, current):
    senders, rows = parts_ref.shape[:2]
    groups, per_group, wide = av_ref.shape
    width = wide - ANGLES
    radii = width // ANGLES
    per_dev = rows // (radii + 1)
    count, classes = senders * per_dev, groups * per_group
    prior = av_ref[:, :, width:].reshape(classes, ANGLES)
    meta = parts_ref[:, radii * per_dev :, :].reshape(count, ANGLES).astype(jnp.float32)
    lane = lax.broadcasted_iota(jnp.int32, (count, ANGLES), 1)
    class_lane = lax.broadcasted_iota(jnp.int32, (count, classes), 1)
    ones = jnp.ones((count, ANGLES), jnp.bfloat16)
    current[...] = av_ref[:, :, :width].reshape(classes, width)

    def value(kind, step):
        return meta[:, kind * STEPS + step : kind * STEPS + step + 1]

    for step in range(STEPS):
        shift = (value(2, step) * ASTEP).astype(jnp.int32)
        label = (value(0, step) * per_group + value(1, step)).astype(jnp.int32)
        index = (lane - shift) & (ANGLES - 1)
        hot = jnp.where(class_lane == label, value(3, step), 0.0).astype(jnp.bfloat16)

        def summed(values):
            return lax.dot_general(hot, values, (((0,), (0,)), ((), ())), preferred_element_type=jnp.float32)

        inverse = 1.0 / (prior + summed(ones))
        for a in range(radii):
            cols = slice(a * ANGLES, (a + 1) * ANGLES)
            image = parts_ref[:, a * per_dev : (a + 1) * per_dev, :].reshape(count, ANGLES).astype(jnp.float32)
            turned = jnp.take_along_axis(image, index, axis=1).astype(jnp.bfloat16)
            current[:, cols] = (prior * current[:, cols] + summed(turned)) * inverse
        start = pl.multiple_of(owners_ref[step] * per_group, per_group)
        refs_ref[step * per_group : (step + 1) * per_group, :] = current[pl.ds(start, per_group), :].astype(jnp.bfloat16)
    last_ref[...] = current[...].astype(jnp.bfloat16).reshape(groups, per_group, width)


def exchange_kernel(doms, groups, blocks_ref, band_ref, mine_ref, got_ref, own_sem, send, recv, b_send, b_recv):
    dom, cls = lax.axis_index("dom"), lax.axis_index("cls")
    devices = doms * groups
    me = dom * groups + cls

    def peer(hop):
        return lax.rem(me + hop, devices)

    def place(device):
        return {"dom": lax.div(device, groups), "cls": lax.rem(device, groups)}

    barrier = pltpu.get_barrier_semaphore()

    @pl.loop(1, devices)
    def _(hop):
        pl.semaphore_signal(barrier, device_id=place(peer(hop)), device_id_type=pl.DeviceIdType.MESH)

    pl.semaphore_wait(barrier, devices - 1)

    def block(hop):
        return pltpu.make_async_remote_copy(
            blocks_ref.at[peer(hop)],
            mine_ref.at[me],
            send.at[hop],
            recv.at[hop],
            place(peer(hop)),
            pl.DeviceIdType.MESH,
        )

    def band(hop):
        other = lax.rem(cls + hop, groups)
        return pltpu.make_async_remote_copy(
            band_ref.at[other],
            got_ref.at[cls],
            b_send.at[hop],
            b_recv.at[hop],
            {"dom": dom, "cls": other},
            pl.DeviceIdType.MESH,
        )

    @pl.loop(1, groups)
    def _(hop):
        band(hop).start()

    @pl.loop(1, devices)
    def _(hop):
        block(hop).start()

    own = [
        pltpu.make_async_copy(blocks_ref.at[me], mine_ref.at[me], own_sem.at[0]),
        pltpu.make_async_copy(band_ref.at[cls], got_ref.at[cls], own_sem.at[1]),
    ]
    for copy in own:
        copy.start()
    for copy in own:
        copy.wait()

    @pl.loop(1, devices)
    def _(hop):
        block(hop).wait()

    @pl.loop(1, groups)
    def _(hop):
        band(hop).wait()


def gather_kernel(
    doms,
    groups,
    refs_ref,
    final_ref,
    images_ref,
    last_ref,
    scores_ref,
    slots_ref,
    rolled,
    total,
    own_sem,
    z_send,
    z_recv,
    r_send,
    r_recv,
    f_send,
    f_recv,
):
    dom, cls = lax.axis_index("dom"), lax.axis_index("cls")
    bits = doms.bit_length() - 1
    per_group, width = final_ref.shape[1:]

    def across(bit):
        return dom + (1 << bit) - (2 << bit) * (lax.div(dom, 1 << bit) % 2)

    def peer(hop):
        return lax.rem(cls + hop, groups)

    barrier = pltpu.get_barrier_semaphore()
    for hop in range(1, groups):
        pl.semaphore_signal(barrier, device_id={"dom": dom, "cls": peer(hop)}, device_id_type=pl.DeviceIdType.MESH)
    for bit in range(bits):
        pl.semaphore_signal(barrier, device_id={"dom": across(bit), "cls": cls}, device_id_type=pl.DeviceIdType.MESH)
    pl.semaphore_wait(barrier, groups - 1 + bits)

    def columns(which_dom, which_cls, count):
        return pl.ds(pl.multiple_of((which_dom * groups + which_cls) * width, width), count * width)

    half_rows = (refs_ref.shape[0] // 2, per_group // 2)
    own = [
        pltpu.make_async_copy(refs_ref, slots_ref.at[dom, cls], own_sem.at[0]),
        pltpu.make_async_copy(final_ref.at[cls], last_ref.at[:, columns(dom, cls, 1)], own_sem.at[1]),
    ]
    for copy in own:
        copy.start()
    z_refs, z_last = [], []
    for hop in range(1, groups):
        target = {"dom": dom, "cls": peer(hop)}
        z_refs.append(
            pltpu.make_async_remote_copy(
                refs_ref, slots_ref.at[dom, cls], z_send.at[0, hop], z_recv.at[0, hop], target, pl.DeviceIdType.MESH
            )
        )
        z_last.append(
            pltpu.make_async_remote_copy(
                final_ref.at[peer(hop)],
                last_ref.at[:, columns(dom, cls, 1)],
                z_send.at[1, hop],
                z_recv.at[1, hop],
                target,
                pl.DeviceIdType.MESH,
            )
        )
    for move in z_refs + z_last:
        move.start()
    for copy in own:
        copy.wait()

    orders = [list(range(1, bits)) + [0], list(range(bits - 1, 0, -1)) + [0]]

    def begin(stage, piece_of, send_sem, recv_sem):
        moves = []
        for half, order in enumerate(orders):
            target = {"dom": across(order[stage]), "cls": cls}
            for pick in range(1 << stage):
                slot = dom
                for place, old in enumerate(order[:stage]):
                    if pick >> place & 1:
                        slot = slot + (1 << old) - (2 << old) * (lax.div(dom, 1 << old) % 2)
                piece = piece_of(half, slot)
                spot = (1 << stage) - 1 + pick
                moves.append(
                    pltpu.make_async_remote_copy(
                        piece, piece, send_sem(half, spot), recv_sem(half, spot), target, pl.DeviceIdType.MESH
                    )
                )
        for move in moves:
            move.start()
        return moves

    def refs_piece(source):
        rows = half_rows[0]
        return lambda half, slot: slots_ref.at[slot, source, half * rows : (half + 1) * rows]

    def last_piece(half, slot):
        rows = half_rows[1]
        return last_ref.at[half * rows : (half + 1) * rows, columns(slot, 0, groups)]

    radii = width // ANGLES
    per_dev = images_ref.shape[1]
    chunks = 8
    depth = images_ref.shape[0] // chunks

    def roll_chunk(chunk):
        part = slice(chunk * depth, (chunk + 1) * depth)
        images = images_ref[part].reshape(depth * per_dev, ANGLES)
        for r in range(ROT):
            turned = pltpu.roll(images, r * ASTEP, 1) if r else images
            rolled[part, r * per_dev : (r + 1) * per_dev, :] = turned.reshape(depth, per_dev, ANGLES)

    def multiply(source, core):
        @pl.loop(0, doms // 4)
        def _(pair):
            picks = [4 * pair + core, 4 * pair + 2 + core]
            views = jnp.concatenate(
                [rolled[(which * groups + source) * radii + j] for which in picks for j in range(radii)], axis=1
            )
            names = jnp.concatenate([slots_ref[which, source] for which in picks], axis=1)
            total[...] += lax.dot_general(
                views, names, (((1,), (1,)), ((), ())), preferred_element_type=jnp.float32
            )

    total[...] = jnp.zeros_like(total)
    todo = list(range(chunks))
    core = lax.rem(dom, 2)
    sent = z_refs + z_last
    flying = [[]] + [[move] for move in z_refs] + [z_last]
    for tick in range(groups + bits):
        for stage in reversed(range(bits)):
            hop = tick - stage
            if hop < 0 or hop > groups:
                continue
            for move in flying[hop]:
                move.wait_recv()
            if hop < groups:
                flying[hop] = begin(
                    stage,
                    refs_piece(lax.rem(cls + groups - hop, groups)),
                    lambda half, spot: r_send.at[hop, half, spot],
                    lambda half, spot: r_recv.at[hop, half, spot],
                )
            else:
                flying[hop] = begin(
                    stage,
                    last_piece,
                    lambda half, spot: f_send.at[half, spot],
                    lambda half, spot: f_recv.at[half, spot],
                )
            sent.extend(flying[hop])
        for chunk in todo[:3]:
            roll_chunk(chunk)
        todo = todo[3:]
        landed = tick - bits + 1
        if 0 <= landed < groups:
            multiply(lax.rem(cls + groups - landed, groups), core)
        if 1 <= landed <= groups:
            for move in flying[landed - 1]:
                move.wait_recv()
            multiply(lax.rem(cls + groups - landed + 1, groups), 1 - core)
    for move in flying[groups]:
        move.wait_recv()

    scale = 1.0 / math.sqrt(RADII * ANGLES)
    pack = ANGLES // per_group
    for q in range(ROT // pack):
        tiles = [total[(q * pack + j) * per_dev : (q * pack + j + 1) * per_dev, :] * scale for j in range(pack)]
        for s in range(STEPS):
            scores_ref[s, :, q * ANGLES : (q + 1) * ANGLES] = jnp.concatenate(
                [t[:, s * per_group : (s + 1) * per_group] for t in tiles], axis=1
            )
    for move in sent:
        move.wait_send()


def per_device(particles, averages, prior_mass, group_ids, class_ids, rot_ids, weights, owners):
    per_dev, pixels = particles.shape
    per_group = averages.shape[0]
    doms, groups = lax.axis_size("dom"), lax.axis_size("cls")
    devices = doms * groups
    width = pixels // devices
    radii = width // ANGLES
    classes = per_group * groups

    meta = jnp.stack([group_ids[:, :, 0], class_ids, rot_ids]).astype(jnp.bfloat16)
    meta = jnp.concatenate([meta, weights[None]]).reshape(4 * STEPS, per_dev).T
    meta = jnp.pad(meta, ((0, 0), (0, ANGLES - 4 * STEPS)))[None]
    images = particles.reshape(per_dev, pixels // ANGLES, ANGLES).transpose(1, 0, 2)
    blocks = images.reshape(devices, radii * per_dev, ANGLES)
    blocks = jnp.concatenate([blocks, jnp.broadcast_to(meta, (devices, per_dev, ANGLES))], axis=1)
    band = lax.dynamic_slice_in_dim(averages, lax.axis_index("dom") * groups * width, groups * width, 1)
    band = band.reshape(per_group, groups, width).transpose(1, 0, 2)
    extra = jnp.broadcast_to(prior_mass[None, :, None], (groups, per_group, ANGLES))
    band = jnp.concatenate([band, extra], axis=2)
    hbm = pl.BlockSpec(memory_space=pl.ANY)
    dma = pltpu.SemaphoreType.DMA
    mine, band = pl.pallas_call(
        functools.partial(exchange_kernel, doms, groups),
        out_shape=(jax.ShapeDtypeStruct(blocks.shape, blocks.dtype), jax.ShapeDtypeStruct(band.shape, band.dtype)),
        in_specs=[hbm, hbm],
        out_specs=(hbm, hbm),
        scratch_shapes=[dma((2,)), dma((devices,)), dma((devices,)), dma((groups,)), dma((groups,))],
        compiler_params=pltpu.CompilerParams(collective_id=1, has_side_effects=True),
        name="exchange",
    )(blocks, band)
    vmem = pl.BlockSpec(memory_space=pltpu.VMEM)
    refs, final = pl.pallas_call(
        update_kernel,
        out_shape=(
            jax.ShapeDtypeStruct((STEPS * per_group, width), jnp.bfloat16),
            jax.ShapeDtypeStruct((groups, per_group, width), jnp.bfloat16),
        ),
        in_specs=[pl.BlockSpec(memory_space=pltpu.SMEM)] + [vmem] * 2,
        out_specs=(vmem, vmem),
        scratch_shapes=[pltpu.VMEM((classes, width), jnp.float32)],
        compiler_params=pltpu.CompilerParams(vmem_limit_bytes=40 * MIB),
        name="update",
    )(owners, mine, band)

    last, scores = pl.pallas_call(
        functools.partial(gather_kernel, doms, groups),
        out_shape=(
            jax.ShapeDtypeStruct((per_group, pixels), jnp.bfloat16),
            jax.ShapeDtypeStruct((STEPS, per_dev, ROT * per_group), jnp.float32),
        ),
        in_specs=[hbm, hbm, vmem],
        out_specs=(hbm, vmem),
        scratch_shapes=[
            pltpu.VMEM((doms, groups, STEPS * per_group, width), jnp.bfloat16),
            pltpu.VMEM((pixels // ANGLES, ROT * per_dev, ANGLES), jnp.bfloat16),
            pltpu.VMEM((ROT * per_dev, STEPS * per_group), jnp.float32),
            dma((2,)),
            dma((2, groups)),
            dma((2, groups)),
            dma((groups, 2, doms)),
            dma((groups, 2, doms)),
            dma((2, doms)),
            dma((2, doms)),
        ],
        compiler_params=pltpu.CompilerParams(
            collective_id=0, has_side_effects=True, vmem_limit_bytes=52 * MIB
        ),
        name="gather_scores",
    )(refs, final, images)
    return scores, last.astype(jnp.float32)


def solution(mesh):
    return jax.shard_map(
        per_device,
        mesh=mesh,
        in_specs=(
            P(("dom", "cls"), None),
            P("cls", None),
            P("cls"),
            P(None, ("dom", "cls"), None),
            P(None, ("dom", "cls")),
            P(None, ("dom", "cls")),
            P(None, ("dom", "cls")),
            P(),
        ),
        out_specs=(P(None, ("dom", "cls"), None), P("cls", None)),
        check_vma=False,
    )
```
